256 devices in a mesh: expert: 64 (over x, z, core), fsdp: 4 (over y).
Axes of the slice: x: 4, y: 4, z: 8, core: 2. Of those that a mesh axis runs over, the one named last changes fastest.
Arguments:
- teacher_in: bfloat16 [8192, 4096], P('expert'), may hold values from -6 to 6
- routes: int32 [8192, 8], P('expert'), may hold values from 0 to 63, all different within a row; in each aligned block of 128 rows (0 to 127, 128 to 255, ...) at most 18 rows name the same one
- route_weights: float32 [8192, 8], P('expert'), may hold values from 0.1 to 0.5
- expert_gate_up: bfloat16 [64, 4096, 2, 1024], P('expert', None, None, 'fsdp'), may hold values from -0.09375 to 0.09375
- expert_down: bfloat16 [64, 1024, 4096], P('expert', 'fsdp'), may hold values from -0.1875 to 0.1875
- student_in: bfloat16 [8192, 2048], P('expert'), may hold values from -16 to 16
- norm_gain: float32 [2048], replicated, may hold values from 0.5 to 2
- projector: bfloat16 [2048, 4096], P(None, 'fsdp'), may hold values from -0.125 to 0.125
- second_moment: float32 [2048, 4096], P('expert', 'fsdp'), may hold values from 2048 to 32768
Outputs:
- d_student: bfloat16 [8192, 2048], P('expert')
- proj_step: float32 [2048, 4096], P('expert', 'fsdp')
The draws below stay inside these ranges and needn't reach their ends.
Inputs may be any that keep to these rules, and one draw needn't show every extreme that they name: `routes`: each row names 8 different experts; in each block of 128 consecutive rows (the rows of one index of expert) no expert is named by more than 18 rows.
All inputs are finite; a program needn't handle non-finite values.
Results may differ from the reference program's by a relative error of at most 0.02.
Values may be sent and summed in bfloat16 or wider, within the bound.
A program may use at most 128 MiB of HBM per device.

```python
import math
import jax
import jax.numpy as jnp
import numpy as np
from jax import lax

DT = 4096
TH = 1024
DS = 2048
TOPK = 8
TG = 128
EXPERTS = 64
CAP = 18
TOKENS = 8192
N_EXPERT = 64
N_FSDP = 4


def strengthened(array, rng, source, target, shards_of, factor):
    owner, partner = [(jnp.arange(array.shape[dim]) // (array.shape[dim] // shards_of)).reshape([-1 if axis == dim else 1 for axis in range(array.ndim)]) for dim in (source, target)]
    chosen = jax.random.permutation(rng, shards_of)[partner]
    strong = (owner == chosen) | (owner == (partner + shards_of // 2) % shards_of)
    return jnp.where(strong, factor * array, array)


def shard_levels(stream_key, shape, shards, low, top_value):
    def one(dim, blocks):
        heights = jax.random.uniform(jax.random.fold_in(jax.random.fold_in(stream_key, 6), dim), (blocks,), jnp.float32, low / len(shards), top_value / len(shards))
        return jnp.repeat(jnp.exp(heights), shape[dim] // blocks).reshape((-1,) + (1,) * (len(shape) - dim - 1))

    loudness = one(*shards[0])
    for cut in shards[1:]:
        loudness = loudness * one(*cut)
    return loudness


def assign_block(rng, own, number, rows, count, top, bound, skew):
    order = jax.random.permutation(rng, count)
    crowded, usual = shares(count, rows * top, bound, skew, True), shares(count, rows * top, bound, skew, False)
    places = jnp.arange(count)

    def named(sizes, turn):
        used = int((sizes > 0).sum())
        fixed = max(1, used // 4)
        passed = fixed + (places - fixed + turn * (used - fixed)) % max(1, count - fixed)
        return jnp.zeros((count,), jnp.int32).at[order[jnp.where(places < fixed, places, passed)]].set(jnp.asarray(sizes, jnp.int32))

    sizes = jnp.where(number % 4 == 0, named(crowded, number // 4), named(usual, number - number // 4 - 1))
    mixed = jax.random.permutation(jax.random.fold_in(own, 3), count)
    donor, receiver = mixed[0:count // 2 * 2:2], mixed[1:count // 2 * 2:2]
    margin = jnp.minimum(sizes[donor] - 1, bound - sizes[receiver]) // 2
    margin = jnp.where((donor == order[0]) | (receiver == order[0]) | (sizes[receiver] == 0), 0, jnp.maximum(margin, 0))
    passed = jax.random.randint(jax.random.fold_in(own, 4), (count // 2,), 0, 1 << 20) % (margin + 1)
    sizes = sizes.at[donor].add(-passed).at[receiver].add(passed)
    labels = jnp.searchsorted(jnp.cumsum(sizes), jnp.arange(rows * top), side="right").astype(jnp.int32)
    listing = labels.reshape(top, rows).T
    listing = listing[jax.random.permutation(jax.random.fold_in(own, 1), rows)]
    turn = jax.random.randint(jax.random.fold_in(own, 2), (rows, 1), 0, top)
    return jnp.take_along_axis(listing, (jnp.arange(top)[None, :] + turn) % top, axis=1)


def shares(count, total, most, skew, full):
    weights = [(1 << 20) // math.isqrt(standing ** skew) + 1 for standing in range(1, count + 1)]
    largest = most if full else min(most, max(-(-total // count), total * weights[0] // sum(weights)))
    least = 1 if total - largest >= count - 1 else 0
    holding, rest = [largest] + [least] * (count - 1), total - largest - least * (count - 1)
    while rest > 0:
        free = [i for i in range(1, count) if holding[i] < largest] or [i for i in range(1, count) if holding[i] < most]
        pool, budget = sum([weights[i] for i in free]), rest
        for i in free:
            more = min(most - holding[i], max(1, budget * weights[i] // pool), rest)
            holding[i] = holding[i] + more
            rest = rest - more
    return np.array(holding)


def noise(stream_key, shape, deviation, limit, pieces=(), kind=jnp.bfloat16):
    loudness = shard_levels(stream_key, shape, pieces, -0.22, 0.18) if pieces else 1.0
    result = jax.random.normal(stream_key, shape, jnp.float32) * deviation * loudness
    return jnp.minimum(jnp.maximum(result, -limit), limit).astype(kind)


def noise_with(own_key, extent, scale, bound, cuts, heavy, kind=jnp.bfloat16):
    drawn = scale * jax.random.normal(own_key, extent, jnp.float32)
    if cuts:
        drawn = drawn * shard_levels(own_key, extent, cuts, -0.22, 0.18)
    return jnp.clip(strengthened(drawn, jax.random.fold_in(own_key, 3), *heavy), -bound, bound).astype(kind)


def setup_inputs(seed: int = 0) -> dict:
    streams_of = jax.random.split(jax.random.key(seed), 10)
    teacher_in = noise(streams_of[0], (TOKENS, DT), 1.0, 6.0, ((0, 64),))
    routes_keys = jax.random.split(jax.random.fold_in(streams_of[1], 1), TOKENS // TG)
    routes_turns = jax.random.permutation(jax.random.fold_in(streams_of[1], 3), TOKENS // TG)
    routes = jax.vmap(lambda own, number: assign_block(jax.random.fold_in(streams_of[1], 2), own, number, TG, EXPERTS, TOPK, CAP, 1))(routes_keys, routes_turns).reshape((TOKENS, TOPK))
    route_weights = jnp.clip(0.1 + 0.4 * jax.random.uniform(streams_of[2], (TOKENS, TOPK), jnp.float32) ** shard_levels(streams_of[2], (TOKENS, TOPK), ((0, 64),), -0.2, 0.2), 0.1, 0.5)
    expert_gate_up = noise(streams_of[3], (EXPERTS, DT, 2, TH), DT ** -0.5, 0.09375, ((0, 64), (3, 4)))
    expert_down = noise(streams_of[4], (EXPERTS, TH, DT), TH ** -0.5, 0.1875, ((0, 64), (1, 4)))
    student_in = noise_with(streams_of[5], (TOKENS, DS), 1.0, 16.0, ((0, 64),), (0, 1, 64, 4.0))
    norm_gain = jnp.clip(jnp.exp(jax.random.uniform(streams_of[6], (DS,), jnp.float32, math.log(0.5), math.log(2.0))), 0.5, 2.0)
    projector = noise(streams_of[7], (DS, DT), DS ** -0.5, 0.125, ((1, 4),))
    second_moment = jnp.clip(jnp.exp(math.log(32768.0) - 2.7725887 * jax.random.uniform(streams_of[8], (DS, DT), jnp.float32) ** shard_levels(streams_of[8], (DS, DT), ((0, 64), (1, 4)), -0.2, 0.2)), 2048.0, 32768.0)
    return {"teacher_in": teacher_in, "routes": routes, "route_weights": route_weights, "expert_gate_up": expert_gate_up, "expert_down": expert_down, "student_in": student_in, "norm_gain": norm_gain, "projector": projector, "second_moment": second_moment}


beta_two = 0.95

def block_targets(block_routes):
    flatten = block_routes.reshape(-1)
    onehot = (flatten[:, None] == jnp.arange(EXPERTS, dtype=jnp.int32)[None, :]).astype(jnp.int32)
    before = jnp.cumsum(onehot, axis=0) - onehot
    position = lax.optimization_barrier(jnp.sum(before * onehot, axis=1))
    return (flatten * CAP + position).astype(jnp.int32)

def expert_block(token_rows, gate_up, down_rows):
    gate_up_out = jnp.dot(token_rows, gate_up.reshape(DT, 2 * TH), preferred_element_type=jnp.float32)
    hidden = (jax.nn.silu(gate_up_out[:, :TH]) * gate_up_out[:, TH:]).astype(jnp.bfloat16)
    block_width = TH // N_FSDP
    summed = jnp.zeros((token_rows.shape[0], DT), jnp.float32)
    for quarter in range(N_FSDP):
        partial_out = jnp.dot(hidden[:, quarter * block_width:(quarter + 1) * block_width], down_rows[quarter * block_width:(quarter + 1) * block_width], preferred_element_type=jnp.float32)
        rounded = lax.optimization_barrier(partial_out.astype(jnp.bfloat16))
        summed = summed + rounded.astype(jnp.float32)
    return summed

def invert_block(target_row, token_row, weight_row):
    slot_token = jnp.full((EXPERTS * CAP,), TOKENS, jnp.int32).at[target_row].set(token_row)
    slot_weight = jnp.zeros((EXPERTS * CAP,), jnp.float32).at[target_row].set(weight_row)
    return (slot_token, slot_weight)

def reference(teacher_in, routes, route_weights, expert_gate_up, expert_down, student_in, norm_gain, projector, second_moment):
    blocks = routes.reshape(N_EXPERT, TG * TOPK)
    targets = jax.vmap(block_targets)(blocks)
    local_token = (jnp.arange(TG * TOPK, dtype=jnp.int32) // TOPK).astype(jnp.int32)
    block_start = (jnp.arange(N_EXPERT, dtype=jnp.int32) * TG).astype(jnp.int32)
    global_token = (local_token[None, :] + block_start[:, None]).astype(jnp.int32)
    weights_flat = route_weights.reshape(N_EXPERT, TG * TOPK)
    slot_token, slot_weight = jax.vmap(invert_block)(targets, global_token, weights_flat)
    slot_token = slot_token.reshape(N_EXPERT, EXPERTS, CAP).transpose(1, 0, 2).reshape(EXPERTS, N_EXPERT * CAP)
    slot_weight = slot_weight.reshape(N_EXPERT, EXPERTS, CAP).transpose(1, 0, 2).reshape(EXPERTS, N_EXPERT * CAP)
    padded = jnp.concatenate([teacher_in, jnp.zeros((1, DT), teacher_in.dtype)], axis=0)

    def one_expert(carry, inputs):
        gate_up, down_rows, tokens_here, weights_here = inputs
        expert_out = expert_block(padded[tokens_here], gate_up, down_rows)
        return (carry.at[tokens_here].add(weights_here[:, None] * expert_out), None)
    teacher, _ = lax.scan(one_expert, jnp.zeros((TOKENS + 1, DT), jnp.float32), (expert_gate_up, expert_down, slot_token, slot_weight))
    teacher = teacher[:TOKENS]
    student_wide = student_in.astype(jnp.float32)
    inv_rms = lax.rsqrt(lax.optimization_barrier(jnp.mean(student_wide * student_wide, axis=1, keepdims=True)) + 1e-06)
    normed = student_wide * inv_rms
    student_feat = (normed * norm_gain[None, :]).astype(jnp.bfloat16)
    residue = (jnp.dot(student_feat, projector, preferred_element_type=jnp.float32) - teacher).astype(jnp.bfloat16)
    feat_grad = jnp.dot(residue, projector.T, preferred_element_type=jnp.float32)
    scaled = feat_grad * norm_gain[None, :]
    d_student = (inv_rms * (scaled - normed * lax.optimization_barrier(jnp.mean(scaled * normed, axis=1, keepdims=True)))).astype(jnp.bfloat16)
    proj_grad = jnp.dot(student_feat.T, residue, preferred_element_type=jnp.float32)
    proj_step = proj_grad / jnp.sqrt(beta_two * second_moment + (1.0 - beta_two) * proj_grad * proj_grad)
    return (d_student, proj_step)
```

```python
import jax
import jax.numpy as jnp
from jax import lax
from jax.sharding import PartitionSpec as P

beta_two = 0.95


def slot_maps(routes, route_weights, experts):
    tokens = routes.shape[0]
    named = routes[:, :, None] == jnp.arange(experts, dtype=jnp.int32)[None, None, :]
    member = jnp.any(named, axis=1)
    weight = jnp.sum(jnp.where(named, route_weights[:, :, None], 0.0), axis=1)
    earlier = jnp.tril(jnp.ones((tokens, tokens), jnp.bfloat16), -1)
    before = jnp.dot(earlier, member.astype(jnp.bfloat16), preferred_element_type=jnp.float32)
    position = jnp.where(member, before.astype(jnp.int32), -1)
    return position.T, weight.T


def per_device(
    teacher_in,
    routes,
    route_weights,
    expert_gate_up,
    expert_down,
    student_in,
    norm_gain,
    projector,
    second_moment,
):
    tokens_here, model_width = teacher_in.shape
    top_count = routes.shape[1]
    experts = lax.axis_size("expert")
    shares = lax.axis_size("fsdp")
    part = model_width // shares
    capacity = min(tokens_here, tokens_here * top_count * 9 // (8 * experts))
    position, weight = slot_maps(routes, route_weights, experts)
    onehot = position[:, None, :] == jnp.arange(capacity, dtype=jnp.int32)[None, :, None]
    select = onehot.astype(jnp.bfloat16)
    weighted = jnp.where(onehot, weight[:, None, :], 0.0)
    high = weighted.astype(jnp.bfloat16)
    low = (weighted - high.astype(jnp.float32)).astype(jnp.bfloat16)
    mine = lax.axis_index("fsdp") * part
    columns = lax.dynamic_slice_in_dim(teacher_in, mine, part, axis=1)
    buffer = jnp.einsum("est,tc->esc", select, columns, preferred_element_type=jnp.float32)
    buffer = buffer.astype(jnp.bfloat16)
    received = lax.all_to_all(buffer, "expert", split_axis=0, concat_axis=0, tiled=True)
    rows = lax.all_gather(received, "fsdp", axis=0)
    down_rows = lax.all_to_all(expert_down[0], "fsdp", split_axis=1, concat_axis=0, tiled=True)
    gate_up = expert_gate_up.reshape(shares, part, -1)
    gate_up_out = jnp.einsum("yesc,ycn->esn", rows, gate_up, preferred_element_type=jnp.float32)
    half = gate_up_out.shape[2] // 2
    hidden = (jax.nn.silu(gate_up_out[:, :, :half]) * gate_up_out[:, :, half:]).astype(jnp.bfloat16)
    hidden_all = lax.all_gather(hidden, "fsdp", axis=0)
    expert_out = jnp.einsum(
        "yesh,yhc->esc",
        hidden_all,
        down_rows.reshape(shares, half, part),
        preferred_element_type=jnp.float32,
    )
    returned = lax.all_to_all(
        expert_out.astype(jnp.bfloat16), "expert", split_axis=0, concat_axis=0, tiled=True
    )
    teacher = jnp.einsum(
        "est,esc->tc", high, returned, preferred_element_type=jnp.float32
    ) + jnp.einsum("est,esc->tc", low, returned, preferred_element_type=jnp.float32)
    student_wide = student_in.astype(jnp.float32)
    inv_rms = lax.rsqrt(jnp.mean(student_wide * student_wide, axis=1, keepdims=True) + 1e-06)
    normed = student_wide * inv_rms
    student_feat = (normed * norm_gain[None, :]).astype(jnp.bfloat16)
    residue = (
        jnp.dot(student_feat, projector, preferred_element_type=jnp.float32) - teacher
    ).astype(jnp.bfloat16)
    feat_part = jnp.einsum("tc,dc->td", residue, projector, preferred_element_type=jnp.float32)
    feat_grad = lax.psum(feat_part.astype(jnp.bfloat16), "fsdp").astype(jnp.float32)
    scaled = feat_grad * norm_gain[None, :]
    d_student = (
        inv_rms * (scaled - normed * jnp.mean(scaled * normed, axis=1, keepdims=True))
    ).astype(jnp.bfloat16)
    grad_block = lax.psum_scatter(
        jnp.einsum("tr,tc->rc", student_feat, residue, preferred_element_type=jnp.float32),
        "expert",
        scatter_dimension=0,
        tiled=True,
    )
    proj_step = grad_block / jnp.sqrt(
        beta_two * second_moment + (1.0 - beta_two) * grad_block * grad_block
    )
    return (d_student, proj_step)


def solution(mesh):
    placed = (
        P("expert", None),
        P("expert", None),
        P("expert", None),
        P("expert", None, None, "fsdp"),
        P("expert", "fsdp", None),
        P("expert", None),
        P(),
        P(None, "fsdp"),
        P("expert", "fsdp"),
    )
    return jax.shard_map(
        per_device,
        mesh=mesh,
        in_specs=placed,
        out_specs=(P("expert", None), P("expert", "fsdp")),
        check_vma=False,
    )
```

```python
import jax
import jax.numpy as jnp
from jax import lax
from jax.experimental import pallas as pl
from jax.experimental.pallas import tpu as pltpu
from jax.sharding import PartitionSpec as P

beta_two = 0.95
MESH = pl.DeviceIdType.MESH
NX, NZ, NY = 4, 8, 4


def remote(src, dst, send_sem, recv_sem, expert, share):
    return pltpu.make_async_remote_copy(
        src_ref=src,
        dst_ref=dst,
        send_sem=send_sem,
        recv_sem=recv_sem,
        device_id=(expert, share),
        device_id_type=MESH,
    )


class Place:
    def __init__(self):
        expert = lax.axis_index("expert")
        self.y = lax.axis_index("fsdp")
        self.x = expert // (2 * NZ)
        self.z = lax.rem(expert // 2, NZ)
        self.k = lax.rem(expert, 2)

    def at(self, dx=0, dz=0, dk=0):
        x = lax.rem(self.x + dx, NX)
        z = lax.rem(self.z + dz, NZ)
        k = lax.rem(self.k + dk, 2)
        return (x * NZ + z) * 2 + k

    def member(self, dx=0, dk=0):
        return lax.rem(self.x + dx, NX) * 2 + lax.rem(self.k + dk, 2)


def meet(place):
    barrier = pltpu.get_barrier_semaphore()
    peers = [(place.at(dx=dx, dk=dk), place.y) for dx in range(NX) for dk in range(2) if dx or dk]
    peers += [(place.at(dz=dz), place.y) for dz in range(1, NZ)]
    peers += [(place.at(), lax.rem(place.y + dy, NY)) for dy in range(1, NY)]
    for peer in peers:
        pl.semaphore_signal(barrier, inc=1, device_id=peer, device_id_type=MESH)
    pl.semaphore_wait(barrier, len(peers))


def finish_kernel(
    teacher_ref,
    student_ref,
    gain_ref,
    projector_ref,
    moment_ref,
    d_ref,
    step_ref,
    feat_ref,
    slab_ref,
    slabs_ref,
    residue_ref,
    part_ref,
    parts_ref,
    d_own,
    d_all,
    grad_ref,
    grads_ref,
    own_grad,
    slab_s,
    slab_r,
    res_s,
    res_r,
    fwd_s,
    fwd_r,
    part_s,
    part_r,
    d_s,
    d_r,
    grad_s,
    grad_r,
):
    place = Place()
    tokens, features = student_ref.shape
    columns = projector_ref.shape[1]
    rows = tokens // NY
    mine = place.member()
    meet(place)

    def norm(wide):
        inv = lax.rsqrt(jnp.mean(wide * wide, axis=1, keepdims=True) + 1e-06)
        return inv, wide * inv

    gain = gain_ref[...]
    feat = norm(student_ref[...].astype(jnp.float32))[1] * gain
    feat_ref[...] = feat.astype(jnp.bfloat16)
    piece = features // (2 * NX * NZ)
    for x in range(NX):
        for z in range(NZ):
            for k in range(2):
                at = ((x * NZ + z) * 2 + k) * piece
                if at % tokens == 0:
                    turned = feat[:, at : at + tokens].T.astype(jnp.bfloat16)
                slab_ref[x * 2 + k, z * piece : (z + 1) * piece, :] = turned[
                    at % tokens : at % tokens + piece
                ]

    sends = []
    slot = pl.ds(pl.multiple_of(mine * tokens, tokens), tokens)
    i = 0
    for dx in range(NX):
        for dk in range(2):
            if dx or dk:
                to = place.at(dx=dx, dk=dk)
                copy = remote(
                    slab_ref.at[place.member(dx, dk)],
                    slabs_ref.at[:, slot],
                    slab_s.at[i],
                    slab_r.at[i],
                    to,
                    place.y,
                )
                copy.start()
                sends.append(copy)
                i += 1
    slabs_ref[:, slot] = slab_ref[mine]

    width = 256

    @pl.loop(0, columns // width)
    def _(n):
        cut = pl.ds(pl.multiple_of(n * width, width), width)
        dense = jnp.dot(feat_ref[...], projector_ref[:, cut], preferred_element_type=jnp.float32)
        residue_ref[slot, cut] = (dense - teacher_ref[:, cut]).astype(jnp.bfloat16)

    def share(i, dx, dk):
        copy = remote(
            residue_ref.at[slot],
            residue_ref.at[slot],
            res_s.at[i],
            res_r.at[i],
            place.at(dx=dx, dk=dk),
            place.y,
        )
        copy.start()
        sends.append(copy)

    share(2, 2, 0)
    share(1, 1, 0)
    share(3, 3, 0)
    share(0, 0, 1)

    @pl.loop(0, features // width)
    def _(n):
        cut = pl.ds(pl.multiple_of(n * width, width), width)
        part_ref[:, cut] = lax.dot_general(
            residue_ref[slot, :],
            projector_ref[cut, :],
            (((1,), (1,)), ((), ())),
            preferred_element_type=jnp.float32,
        ).astype(jnp.bfloat16)

    for dy in (2, 1, 3):
        to = lax.rem(place.y + dy, NY)
        copy = remote(
            part_ref.at[pl.ds(pl.multiple_of(to * rows, rows), rows)],
            parts_ref.at[dy - 1],
            part_s.at[dy - 1],
            part_r.at[dy - 1],
            place.at(),
            to,
        )
        copy.start()
        sends.append(copy)

    def landed(ref, send_sem, recv_sem):
        remote(ref, ref, send_sem, recv_sem, place.at(), place.y).wait_recv()

    for dx in (1, 3, 2):
        source = lax.rem(place.x + NX - dx, NX) * 2 + place.k
        arrived = residue_ref.at[pl.ds(pl.multiple_of(source * tokens, tokens), tokens)]
        landed(arrived, res_s.at[dx], res_r.at[dx])
        copy = remote(
            arrived, arrived, fwd_s.at[dx - 1], fwd_r.at[dx - 1], place.at(dk=1), place.y
        )
        copy.start()
        sends.append(copy)

    own_rows = pl.ds(pl.multiple_of(place.y * rows, rows), rows)
    feat_grad = part_ref[own_rows, :].astype(jnp.float32)
    for dy in range(1, NY):
        landed(parts_ref.at[dy - 1], part_s.at[dy - 1], part_r.at[dy - 1])
        feat_grad += parts_ref[dy - 1].astype(jnp.float32)
    inv, normed = norm(student_ref[own_rows, :].astype(jnp.float32))
    scaled = feat_grad * gain
    d_own[...] = (
        inv * (scaled - normed * jnp.mean(scaled * normed, axis=1, keepdims=True))
    ).astype(jnp.bfloat16)
    for dy in (2, 1, 3):
        copy = remote(
            d_own,
            d_all.at[dy - 1],
            d_s.at[dy - 1],
            d_r.at[dy - 1],
            place.at(),
            lax.rem(place.y + dy, NY),
        )
        copy.start()
        sends.append(copy)
    d_ref[own_rows, :] = d_own[...]

    i = 0
    for dx in range(NX):
        for dk in range(2):
            if dx or dk:
                source = place.member(NX - dx, dk)
                at = pl.ds(pl.multiple_of(source * tokens, tokens), tokens)
                landed(slabs_ref.at[:, at], slab_s.at[i], slab_r.at[i])
                i += 1
    other = 1 - place.k
    partner = pl.ds(pl.multiple_of((place.x * 2 + other) * tokens, tokens), tokens)
    landed(residue_ref.at[partner], res_s.at[0], res_r.at[0])
    for dx in (1, 3, 2):
        source = lax.rem(place.x + NX - dx, NX) * 2 + other
        at = pl.ds(pl.multiple_of(source * tokens, tokens), tokens)
        landed(residue_ref.at[at], fwd_s.at[dx - 1], fwd_r.at[dx - 1])

    @pl.loop(0, columns // width)
    def _(n):
        cut = pl.ds(pl.multiple_of(n * width, width), width)
        grad = jnp.dot(slabs_ref[...], residue_ref[:, cut], preferred_element_type=jnp.float32)
        grad = grad.reshape(NZ, piece, width)
        grad_ref[:, :, cut] = grad.astype(jnp.bfloat16)
        own_grad[:, :, cut] = grad

    for dz in (4, 3, 5, 2, 6, 1, 7):
        copy = remote(
            grad_ref.at[lax.rem(place.z + dz, NZ)],
            grads_ref.at[dz - 1],
            grad_s.at[dz - 1],
            grad_r.at[dz - 1],
            place.at(dz=dz),
            place.y,
        )
        copy.start()
        sends.append(copy)
    for dy in range(1, NY):
        source = lax.rem(place.y + NY - dy, NY)
        landed(d_all.at[dy - 1], d_s.at[dy - 1], d_r.at[dy - 1])
        d_ref[pl.ds(pl.multiple_of(source * rows, rows), rows), :] = d_all[dy - 1]
    total = own_grad[place.z]
    for dz in (1, 7, 2, 6, 3, 5, 4):
        landed(grads_ref.at[dz - 1], grad_s.at[dz - 1], grad_r.at[dz - 1])
        total += grads_ref[dz - 1].astype(jnp.float32)
    step_ref[...] = total * lax.rsqrt(
        beta_two * moment_ref[...] + (1.0 - beta_two) * total * total
    )
    for copy in sends:
        copy.wait_send()


def finish(teacher, student_in, norm_gain, projector, second_moment):
    tokens, features = student_in.shape
    columns = projector.shape[1]
    rows = tokens // NY
    piece = features // (2 * NX * NZ)
    dma = pltpu.SemaphoreType.DMA
    bf16, f32 = jnp.bfloat16, jnp.float32
    return pl.pallas_call(
        finish_kernel,
        out_shape=(
            jax.ShapeDtypeStruct((tokens, features), bf16),
            jax.ShapeDtypeStruct(second_moment.shape, f32),
        ),
        in_specs=[pl.BlockSpec(memory_space=pltpu.VMEM)] * 5,
        out_specs=[pl.BlockSpec(memory_space=pltpu.VMEM)] * 2,
        scratch_shapes=[
            pltpu.VMEM((tokens, features), bf16),
            pltpu.VMEM((2 * NX, NZ * piece, tokens), bf16),
            pltpu.VMEM((NZ * piece, 2 * NX * tokens), bf16),
            pltpu.VMEM((2 * NX * tokens, columns), bf16),
            pltpu.VMEM((tokens, features), bf16),
            pltpu.VMEM((NY - 1, rows, features), bf16),
            pltpu.VMEM((rows, features), bf16),
            pltpu.VMEM((NY - 1, rows, features), bf16),
            pltpu.VMEM((NZ, piece, columns), bf16),
            pltpu.VMEM((NZ - 1, piece, columns), bf16),
            pltpu.VMEM((NZ, piece, columns), f32),
        ]
        + [dma((n,)) for n in (7, 7, 4, 4, 3, 3, 3, 3, 3, 3, 7, 7)],
        compiler_params=pltpu.CompilerParams(
            collective_id=1, has_side_effects=True, vmem_limit_bytes=48 << 20
        ),
    )(teacher, student_in, norm_gain.reshape(1, -1), projector, second_moment)


def slot_maps(routes, route_weights, experts):
    tokens = routes.shape[0]
    named = routes[:, :, None] == jnp.arange(experts, dtype=jnp.int32)[None, None, :]
    member = jnp.any(named, axis=1)
    weight = jnp.sum(jnp.where(named, route_weights[:, :, None], 0.0), axis=1)
    earlier = jnp.tril(jnp.ones((tokens, tokens), jnp.bfloat16), -1)
    before = jnp.dot(earlier, member.astype(jnp.bfloat16), preferred_element_type=jnp.float32)
    position = jnp.where(member, before.astype(jnp.int32), -1)
    return position.T, weight.T


def per_device(
    teacher_in,
    routes,
    route_weights,
    expert_gate_up,
    expert_down,
    student_in,
    norm_gain,
    projector,
    second_moment,
):
    tokens_here, model_width = teacher_in.shape
    top_count = routes.shape[1]
    experts = lax.axis_size("expert")
    shares = lax.axis_size("fsdp")
    part = model_width // shares
    capacity = min(tokens_here, tokens_here * top_count * 9 // (8 * experts))
    position, weight = slot_maps(routes, route_weights, experts)
    onehot = position[:, None, :] == jnp.arange(capacity, dtype=jnp.int32)[None, :, None]
    select = onehot.astype(jnp.bfloat16)
    weighted = jnp.where(onehot, weight[:, None, :], 0.0)
    high = weighted.astype(jnp.bfloat16)
    low = (weighted - high.astype(jnp.float32)).astype(jnp.bfloat16)
    mine = lax.axis_index("fsdp") * part
    columns = lax.dynamic_slice_in_dim(teacher_in, mine, part, axis=1)
    buffer = jnp.einsum("est,tc->esc", select, columns, preferred_element_type=jnp.float32)
    buffer = buffer.astype(jnp.bfloat16)
    received = lax.all_to_all(buffer, "expert", split_axis=0, concat_axis=0, tiled=True)
    rows = lax.all_gather(received, "fsdp", axis=0)
    down_rows = lax.all_to_all(expert_down[0], "fsdp", split_axis=1, concat_axis=0, tiled=True)
    gate_up = expert_gate_up.reshape(shares, part, -1)
    gate_up_out = jnp.einsum("yesc,ycn->esn", rows, gate_up, preferred_element_type=jnp.float32)
    half = gate_up_out.shape[2] // 2
    hidden = (jax.nn.silu(gate_up_out[:, :, :half]) * gate_up_out[:, :, half:]).astype(jnp.bfloat16)
    hidden_all = lax.all_gather(hidden, "fsdp", axis=0)
    expert_out = jnp.einsum(
        "yesh,yhc->esc",
        hidden_all,
        down_rows.reshape(shares, half, part),
        preferred_element_type=jnp.float32,
    )
    returned = lax.all_to_all(
        expert_out.astype(jnp.bfloat16), "expert", split_axis=0, concat_axis=0, tiled=True
    )
    teacher = jnp.einsum(
        "est,esc->tc", high, returned, preferred_element_type=jnp.float32
    ) + jnp.einsum("est,esc->tc", low, returned, preferred_element_type=jnp.float32)
    return finish(teacher, student_in, norm_gain, projector, second_moment)


def solution(mesh):
    placed = (
        P("expert", None),
        P("expert", None),
        P("expert", None),
        P("expert", None, None, "fsdp"),
        P("expert", "fsdp", None),
        P("expert", None),
        P(),
        P(None, "fsdp"),
        P("expert", "fsdp"),
    )
    return jax.shard_map(
        per_device,
        mesh=mesh,
        in_specs=placed,
        out_specs=(P("expert", None), P("expert", "fsdp")),
        check_vma=False,
    )
```

```python
import jax
import jax.numpy as jnp
from jax import lax
from jax.experimental import pallas as pl
from jax.experimental.pallas import tpu as pltpu
from jax.sharding import PartitionSpec as P

beta_two = 0.95
MESH = pl.DeviceIdType.MESH
NX, NZ, NY = 4, 8, 4


def remote(src, dst, send_sem, recv_sem, expert, share):
    return pltpu.make_async_remote_copy(
        src_ref=src,
        dst_ref=dst,
        send_sem=send_sem,
        recv_sem=recv_sem,
        device_id=(expert, share),
        device_id_type=MESH,
    )


class Place:
    def __init__(self):
        expert = lax.axis_index("expert")
        self.y = lax.axis_index("fsdp")
        self.x = expert // (2 * NZ)
        self.z = lax.rem(expert // 2, NZ)
        self.k = lax.rem(expert, 2)

    def at(self, dx=0, dz=0, dk=0):
        x = lax.rem(self.x + dx, NX)
        z = lax.rem(self.z + dz, NZ)
        k = lax.rem(self.k + dk, 2)
        return (x * NZ + z) * 2 + k

    def member(self, dx=0, dk=0):
        return lax.rem(self.x + dx, NX) * 2 + lax.rem(self.k + dk, 2)


def meet(place):
    barrier = pltpu.get_barrier_semaphore()
    peers = [(place.at(dx=dx, dk=dk), place.y) for dx in range(NX) for dk in range(2) if dx or dk]
    peers += [(place.at(dz=dz), place.y) for dz in range(1, NZ)]
    peers += [(place.at(), lax.rem(place.y + dy, NY)) for dy in range(1, NY)]
    for peer in peers:
        pl.semaphore_signal(barrier, inc=1, device_id=peer, device_id_type=MESH)
    pl.semaphore_wait(barrier, len(peers))


def experts_kernel(
    teacher_in_ref,
    meta_ref,
    gate_up_ref,
    down_ref,
    out_ref,
    tok_ref,
    metas_ref,
    select_ref,
    spread_ref,
    send_ref,
    rows_ref,
    hidden_ref,
    down_all,
    back_ref,
    home_ref,
    half_ref,
    half_in,
    total_ref,
    third_ref,
    third_in,
    tok_s,
    tok_r,
    meta_s,
    meta_r,
    tokf_s,
    tokf_r,
    metaf_s,
    metaf_r,
    down_s,
    down_r,
    z_s,
    z_r,
    up_s,
    up_r,
    low_s,
    low_r,
    relay_s,
    relay_r,
    hid_s,
    hid_r,
    ret_s,
    ret_r,
    half_s,
    half_r,
    third_s,
    third_r,
):
    place = Place()
    tokens = teacher_in_ref.shape[0]
    part = out_ref.shape[1]
    units = down_ref.shape[0]
    block = rows_ref.shape[2]
    f32, bf16 = jnp.float32, jnp.bfloat16
    y = place.y
    mine = place.member()
    meet(place)
    sends = []

    def send(*args):
        copy = remote(*args)
        copy.start()
        sends.append(copy)

    def landed(ref, send_sem, recv_sem):
        remote(ref, ref, send_sem, recv_sem, place.at(), y).wait_recv()

    def tok_slot(member):
        return tok_ref.at[pl.ds(pl.multiple_of(member * tokens, tokens), tokens)]

    def share_columns(share):
        return pl.ds(pl.multiple_of(share * part, part), part)

    own = teacher_in_ref.at[:, share_columns(y)]
    for i, dx, dk in ((1, 1, 0), (3, 3, 0), (2, 2, 0), (0, 0, 1)):
        to = place.at(dx=dx, dk=dk)
        send(meta_ref, metas_ref.at[mine], meta_s.at[i], meta_r.at[i], to, y)
        send(own, tok_slot(mine), tok_s.at[i], tok_r.at[i], to, y)
    for dy in (2, 1, 3):
        to = lax.rem(y + dy, NY)
        send(
            down_ref.at[:, share_columns(to)],
            down_all.at[dy],
            down_s.at[dy - 1],
            down_r.at[dy - 1],
            place.at(),
            to,
        )
    tok_ref[pl.ds(pl.multiple_of(mine * tokens, tokens), tokens), :] = teacher_in_ref[
        :, share_columns(y)
    ]
    metas_ref[mine] = meta_ref[...]
    down_all[0] = down_ref[:, share_columns(y)]
    for dx in (1, 3, 2):
        source = place.member(NX - dx)
        landed(metas_ref.at[source], meta_s.at[dx], meta_r.at[dx])
        send(
            metas_ref.at[source],
            metas_ref.at[source],
            metaf_s.at[dx - 1],
            metaf_r.at[dx - 1],
            place.at(dk=1),
            y,
        )
        landed(tok_slot(source), tok_s.at[dx], tok_r.at[dx])
        send(
            tok_slot(source),
            tok_slot(source),
            tokf_s.at[dx - 1],
            tokf_r.at[dx - 1],
            place.at(dk=1),
            y,
        )
    landed(metas_ref.at[place.member(0, 1)], meta_s.at[0], meta_r.at[0])
    landed(tok_slot(place.member(0, 1)), tok_s.at[0], tok_r.at[0])
    for dx in (1, 3, 2):
        source = place.member(NX - dx, 1)
        landed(metas_ref.at[source], metaf_s.at[dx - 1], metaf_r.at[dx - 1])
        landed(tok_slot(source), tokf_s.at[dx - 1], tokf_r.at[dx - 1])

    number = lax.broadcasted_iota(jnp.int32, (block, tokens), 0).astype(f32)
    order = (0, 1, 7, 2, 6, 3, 5, 4)

    for dz in order:
        expert = place.at(dz=dz)
        for o in range(2 * NX):
            code = metas_ref[o, 0, pl.ds(expert, 1), :]
            select_ref[:, o * tokens : (o + 1) * tokens] = jnp.where(
                number == code, 1.0, 0.0
            ).astype(bf16)
        picked = jnp.dot(select_ref[...], tok_ref[...], preferred_element_type=f32).astype(bf16)
        if dz == 0:
            rows_ref[0, 0] = picked
        else:
            send_ref[dz - 1] = picked
            send(
                send_ref.at[dz - 1],
                rows_ref.at[0, dz],
                z_s.at[dz - 1],
                z_r.at[dz - 1],
                expert,
                y,
            )

    after, ahead = lax.rem(y + 1, NY), lax.rem(y + NY - 1, NY)

    def pass_rows(j):
        dz = order[j]
        if dz:
            landed(rows_ref.at[0, dz], z_s.at[dz - 1], z_r.at[dz - 1])
        send(rows_ref.at[0, dz], rows_ref.at[1, dz], up_s.at[dz], up_r.at[dz], place.at(), after)
        send(rows_ref.at[0, dz], rows_ref.at[3, dz], low_s.at[dz], low_r.at[dz], place.at(), ahead)

    def relay_rows(j):
        dz = order[j]
        landed(rows_ref.at[1, dz], up_s.at[dz], up_r.at[dz])
        landed(rows_ref.at[3, dz], low_s.at[dz], low_r.at[dz])
        source, to = (1, after) if j % 2 == 0 else (3, ahead)
        send(
            rows_ref.at[source, dz],
            rows_ref.at[2, dz],
            relay_s.at[dz],
            relay_r.at[dz],
            place.at(),
            to,
        )

    def first_product(j):
        dz = order[j]
        landed(rows_ref.at[2, dz], relay_s.at[dz], relay_r.at[dz])
        out = jnp.zeros((block, 2 * units), f32)
        for ry in range(NY):
            share = lax.rem(y + NY - ry, NY)
            out += jnp.dot(
                rows_ref[ry, dz],
                gate_up_ref[share_columns(share), :],
                preferred_element_type=f32,
            )
        gate, up = out[:, :units], out[:, units:]
        hidden_ref[0, dz] = (gate / (1.0 + jnp.exp(-gate)) * up).astype(bf16)
        for dy in (2, 1, 3):
            send(
                hidden_ref.at[0, dz],
                hidden_ref.at[dy, dz],
                hid_s.at[dy - 1, dz],
                hid_r.at[dy - 1, dz],
                place.at(),
                lax.rem(y + dy, NY),
            )

    def second_product(j):
        dz = order[j]
        for dy in range(1, NY):
            landed(hidden_ref.at[dy, dz], hid_s.at[dy - 1, dz], hid_r.at[dy - 1, dz])
        out = jnp.zeros((block, part), f32)
        for ry in range(NY):
            out += jnp.dot(hidden_ref[ry, dz], down_all[ry], preferred_element_type=f32)
        if dz == 0:
            home_ref[0:block, :] = out.astype(bf16)
        else:
            back_ref[dz - 1] = out.astype(bf16)
            send(
                back_ref.at[dz - 1],
                home_ref.at[dz * block : (dz + 1) * block],
                ret_s.at[dz - 1],
                ret_r.at[dz - 1],
                place.at(dz=NZ - dz),
                y,
            )

    def weigh():
        for dk in (1, 0):
            for dx in range(NX):
                o = place.member(dx, dk)
                pieces = []
                for dz in range(NZ):
                    expert = pl.ds(place.at(dz=dz), 1)
                    pieces.append(
                        jnp.where(number == metas_ref[o, 0, expert, :], metas_ref[o, 1, expert, :], 0.0)
                    )
                at = ((1 - dk) * NX + dx) * tokens
                spread_ref[at : at + tokens, :] = jnp.concatenate(pieces, axis=0).T.astype(bf16)

    steps = len(order)
    pass_rows(0)
    weigh()
    for dy in range(1, NY):
        landed(down_all.at[dy], down_s.at[dy - 1], down_r.at[dy - 1])
    for j in range(1, steps + 4):
        if j < steps:
            pass_rows(j)
        if 0 <= j - 1 < steps:
            relay_rows(j - 1)
        if 0 <= j - 2 < steps:
            first_product(j - 2)
        if 0 <= j - 4 < steps:
            second_product(j - 4)

    for dz in order[1:]:
        landed(home_ref.at[dz * block : (dz + 1) * block], ret_s.at[dz - 1], ret_r.at[dz - 1])
    width = 256
    count = NX * tokens

    @pl.loop(0, part // width)
    def _(n):
        cut = pl.ds(pl.multiple_of(n * width, width), width)
        half_ref[:, cut] = jnp.dot(
            spread_ref[:count, :], home_ref[:, cut], preferred_element_type=f32
        ).astype(bf16)

    send(half_ref, half_in, half_s.at[0], half_r.at[0], place.at(dk=1), y)

    @pl.loop(0, part // width)
    def _(n):
        cut = pl.ds(pl.multiple_of(n * width, width), width)
        total_ref[:, cut] = jnp.dot(
            spread_ref[count:, :], home_ref[:, cut], preferred_element_type=f32
        )

    landed(half_in, half_s.at[0], half_r.at[0])
    for dx in (2, 1, 3):
        at = slice(dx * tokens, (dx + 1) * tokens)
        third_ref[dx - 1] = (total_ref[at, :] + half_in[at, :].astype(f32)).astype(bf16)
        send(
            third_ref.at[dx - 1],
            third_in.at[dx - 1],
            third_s.at[dx - 1],
            third_r.at[dx - 1],
            place.at(dx=dx),
            y,
        )
    teacher = total_ref[:tokens, :] + half_in[:tokens, :].astype(f32)
    for dx in (1, 3, 2):
        landed(third_in.at[dx - 1], third_s.at[dx - 1], third_r.at[dx - 1])
        teacher += third_in[dx - 1].astype(f32)
    out_ref[...] = teacher
    for copy in sends:
        copy.wait_send()


def experts_output(teacher_in, meta, gate_up, down, capacity):
    tokens, width = teacher_in.shape
    part = width // NY
    units = down.shape[0]
    oct_size = 2 * NX
    block = oct_size * capacity
    dma = pltpu.SemaphoreType.DMA
    bf16, f32 = jnp.bfloat16, jnp.float32
    return pl.pallas_call(
        experts_kernel,
        out_shape=jax.ShapeDtypeStruct((tokens, part), f32),
        in_specs=[pl.BlockSpec(memory_space=pltpu.VMEM)] * 4,
        out_specs=pl.BlockSpec(memory_space=pltpu.VMEM),
        scratch_shapes=[
            pltpu.VMEM((oct_size * tokens, part), bf16),
            pltpu.VMEM((oct_size,) + meta.shape, f32),
            pltpu.VMEM((block, oct_size * tokens), bf16),
            pltpu.VMEM((oct_size * tokens, NZ * block), bf16),
            pltpu.VMEM((NZ - 1, block, part), bf16),
            pltpu.VMEM((NY, NZ, block, part), bf16),
            pltpu.VMEM((NY, NZ, block, units), bf16),
            pltpu.VMEM((NY, units, part), bf16),
            pltpu.VMEM((NZ - 1, block, part), bf16),
            pltpu.VMEM((NZ * block, part), bf16),
            pltpu.VMEM((NX * tokens, part), bf16),
            pltpu.VMEM((NX * tokens, part), bf16),
            pltpu.VMEM((NX * tokens, part), f32),
            pltpu.VMEM((NX - 1, tokens, part), bf16),
            pltpu.VMEM((NX - 1, tokens, part), bf16),
        ]
        + [
            dma(n)
            for n in (
                [(4,)] * 4 + [(3,)] * 4 + [(3,)] * 2 + [(7,)] * 2 + [(8,)] * 6
                + [(3, 8)] * 2 + [(7,)] * 2 + [(1,)] * 2 + [(3,)] * 2
            )
        ],
        compiler_params=pltpu.CompilerParams(
            collective_id=0, has_side_effects=True, vmem_limit_bytes=58 << 20
        ),
    )(teacher_in, meta, gate_up, down)


def finish_kernel(
    teacher_ref,
    student_ref,
    gain_ref,
    projector_ref,
    moment_ref,
    d_ref,
    step_ref,
    feat_ref,
    slab_ref,
    slabs_ref,
    residue_ref,
    part_ref,
    parts_ref,
    d_own,
    d_all,
    grad_ref,
    grads_ref,
    own_grad,
    slab_s,
    slab_r,
    res_s,
    res_r,
    fwd_s,
    fwd_r,
    part_s,
    part_r,
    d_s,
    d_r,
    grad_s,
    grad_r,
):
    place = Place()
    tokens, features = student_ref.shape
    columns = projector_ref.shape[1]
    rows = tokens // NY
    mine = place.member()
    meet(place)

    def norm(wide):
        inv = lax.rsqrt(jnp.mean(wide * wide, axis=1, keepdims=True) + 1e-06)
        return inv, wide * inv

    gain = gain_ref[...]
    feat = norm(student_ref[...].astype(jnp.float32))[1] * gain
    feat_ref[...] = feat.astype(jnp.bfloat16)
    piece = features // (2 * NX * NZ)
    for x in range(NX):
        for z in range(NZ):
            for k in range(2):
                at = ((x * NZ + z) * 2 + k) * piece
                if at % tokens == 0:
                    turned = feat[:, at : at + tokens].T.astype(jnp.bfloat16)
                slab_ref[x * 2 + k, z * piece : (z + 1) * piece, :] = turned[
                    at % tokens : at % tokens + piece
                ]

    sends = []
    slot = pl.ds(pl.multiple_of(mine * tokens, tokens), tokens)
    i = 0
    for dx in range(NX):
        for dk in range(2):
            if dx or dk:
                to = place.at(dx=dx, dk=dk)
                copy = remote(
                    slab_ref.at[place.member(dx, dk)],
                    slabs_ref.at[:, slot],
                    slab_s.at[i],
                    slab_r.at[i],
                    to,
                    place.y,
                )
                copy.start()
                sends.append(copy)
                i += 1
    slabs_ref[:, slot] = slab_ref[mine]

    width = 256

    @pl.loop(0, columns // width)
    def _(n):
        cut = pl.ds(pl.multiple_of(n * width, width), width)
        dense = jnp.dot(feat_ref[...], projector_ref[:, cut], preferred_element_type=jnp.float32)
        residue_ref[slot, cut] = (dense - teacher_ref[:, cut]).astype(jnp.bfloat16)

    def share(i, dx, dk):
        copy = remote(
            residue_ref.at[slot],
            residue_ref.at[slot],
            res_s.at[i],
            res_r.at[i],
            place.at(dx=dx, dk=dk),
            place.y,
        )
        copy.start()
        sends.append(copy)

    share(2, 2, 0)
    share(1, 1, 0)
    share(3, 3, 0)
    share(0, 0, 1)

    @pl.loop(0, features // width)
    def _(n):
        cut = pl.ds(pl.multiple_of(n * width, width), width)
        part_ref[:, cut] = lax.dot_general(
            residue_ref[slot, :],
            projector_ref[cut, :],
            (((1,), (1,)), ((), ())),
            preferred_element_type=jnp.float32,
        ).astype(jnp.bfloat16)

    for dy in (2, 1, 3):
        to = lax.rem(place.y + dy, NY)
        copy = remote(
            part_ref.at[pl.ds(pl.multiple_of(to * rows, rows), rows)],
            parts_ref.at[dy - 1],
            part_s.at[dy - 1],
            part_r.at[dy - 1],
            place.at(),
            to,
        )
        copy.start()
        sends.append(copy)

    def landed(ref, send_sem, recv_sem):
        remote(ref, ref, send_sem, recv_sem, place.at(), place.y).wait_recv()

    for dx in (1, 3, 2):
        source = lax.rem(place.x + NX - dx, NX) * 2 + place.k
        arrived = residue_ref.at[pl.ds(pl.multiple_of(source * tokens, tokens), tokens)]
        landed(arrived, res_s.at[dx], res_r.at[dx])
        copy = remote(
            arrived, arrived, fwd_s.at[dx - 1], fwd_r.at[dx - 1], place.at(dk=1), place.y
        )
        copy.start()
        sends.append(copy)

    own_rows = pl.ds(pl.multiple_of(place.y * rows, rows), rows)
    feat_grad = part_ref[own_rows, :].astype(jnp.float32)
    for dy in range(1, NY):
        landed(parts_ref.at[dy - 1], part_s.at[dy - 1], part_r.at[dy - 1])
        feat_grad += parts_ref[dy - 1].astype(jnp.float32)
    inv, normed = norm(student_ref[own_rows, :].astype(jnp.float32))
    scaled = feat_grad * gain
    d_own[...] = (
        inv * (scaled - normed * jnp.mean(scaled * normed, axis=1, keepdims=True))
    ).astype(jnp.bfloat16)
    for dy in (2, 1, 3):
        copy = remote(
            d_own,
            d_all.at[dy - 1],
            d_s.at[dy - 1],
            d_r.at[dy - 1],
            place.at(),
            lax.rem(place.y + dy, NY),
        )
        copy.start()
        sends.append(copy)
    d_ref[own_rows, :] = d_own[...]

    i = 0
    for dx in range(NX):
        for dk in range(2):
            if dx or dk:
                source = place.member(NX - dx, dk)
                at = pl.ds(pl.multiple_of(source * tokens, tokens), tokens)
                landed(slabs_ref.at[:, at], slab_s.at[i], slab_r.at[i])
                i += 1
    other = 1 - place.k
    partner = pl.ds(pl.multiple_of((place.x * 2 + other) * tokens, tokens), tokens)
    landed(residue_ref.at[partner], res_s.at[0], res_r.at[0])
    for dx in (1, 3, 2):
        source = lax.rem(place.x + NX - dx, NX) * 2 + other
        at = pl.ds(pl.multiple_of(source * tokens, tokens), tokens)
        landed(residue_ref.at[at], fwd_s.at[dx - 1], fwd_r.at[dx - 1])

    @pl.loop(0, columns // width)
    def _(n):
        cut = pl.ds(pl.multiple_of(n * width, width), width)
        grad = jnp.dot(slabs_ref[...], residue_ref[:, cut], preferred_element_type=jnp.float32)
        grad = grad.reshape(NZ, piece, width)
        grad_ref[:, :, cut] = grad.astype(jnp.bfloat16)
        own_grad[:, :, cut] = grad

    for dz in (4, 3, 5, 2, 6, 1, 7):
        copy = remote(
            grad_ref.at[lax.rem(place.z + dz, NZ)],
            grads_ref.at[dz - 1],
            grad_s.at[dz - 1],
            grad_r.at[dz - 1],
            place.at(dz=dz),
            place.y,
        )
        copy.start()
        sends.append(copy)
    for dy in range(1, NY):
        source = lax.rem(place.y + NY - dy, NY)
        landed(d_all.at[dy - 1], d_s.at[dy - 1], d_r.at[dy - 1])
        d_ref[pl.ds(pl.multiple_of(source * rows, rows), rows), :] = d_all[dy - 1]
    total = own_grad[place.z]
    for dz in (1, 7, 2, 6, 3, 5, 4):
        landed(grads_ref.at[dz - 1], grad_s.at[dz - 1], grad_r.at[dz - 1])
        total += grads_ref[dz - 1].astype(jnp.float32)
    step_ref[...] = total * lax.rsqrt(
        beta_two * moment_ref[...] + (1.0 - beta_two) * total * total
    )
    for copy in sends:
        copy.wait_send()


def finish(teacher, student_in, norm_gain, projector, second_moment):
    tokens, features = student_in.shape
    columns = projector.shape[1]
    rows = tokens // NY
    piece = features // (2 * NX * NZ)
    dma = pltpu.SemaphoreType.DMA
    bf16, f32 = jnp.bfloat16, jnp.float32
    return pl.pallas_call(
        finish_kernel,
        out_shape=(
            jax.ShapeDtypeStruct((tokens, features), bf16),
            jax.ShapeDtypeStruct(second_moment.shape, f32),
        ),
        in_specs=[pl.BlockSpec(memory_space=pltpu.VMEM)] * 5,
        out_specs=[pl.BlockSpec(memory_space=pltpu.VMEM)] * 2,
        scratch_shapes=[
            pltpu.VMEM((tokens, features), bf16),
            pltpu.VMEM((2 * NX, NZ * piece, tokens), bf16),
            pltpu.VMEM((NZ * piece, 2 * NX * tokens), bf16),
            pltpu.VMEM((2 * NX * tokens, columns), bf16),
            pltpu.VMEM((tokens, features), bf16),
            pltpu.VMEM((NY - 1, rows, features), bf16),
            pltpu.VMEM((rows, features), bf16),
            pltpu.VMEM((NY - 1, rows, features), bf16),
            pltpu.VMEM((NZ, piece, columns), bf16),
            pltpu.VMEM((NZ - 1, piece, columns), bf16),
            pltpu.VMEM((NZ, piece, columns), f32),
        ]
        + [dma((n,)) for n in (7, 7, 4, 4, 3, 3, 3, 3, 3, 3, 7, 7)],
        compiler_params=pltpu.CompilerParams(
            collective_id=1, has_side_effects=True, vmem_limit_bytes=48 << 20
        ),
    )(teacher, student_in, norm_gain.reshape(1, -1), projector, second_moment)


def slot_maps(routes, route_weights, experts):
    tokens = routes.shape[0]
    named = routes[:, :, None] == jnp.arange(experts, dtype=jnp.int32)[None, None, :]
    member = jnp.any(named, axis=1)
    weight = jnp.sum(jnp.where(named, route_weights[:, :, None], 0.0), axis=1)
    earlier = jnp.tril(jnp.ones((tokens, tokens), jnp.bfloat16), -1)
    before = jnp.dot(earlier, member.astype(jnp.bfloat16), preferred_element_type=jnp.float32)
    position = jnp.where(member, before.astype(jnp.int32), -1)
    return position.T, weight.T


def per_device(
    teacher_in,
    routes,
    route_weights,
    expert_gate_up,
    expert_down,
    student_in,
    norm_gain,
    projector,
    second_moment,
):
    tokens_here = teacher_in.shape[0]
    top_count = routes.shape[1]
    experts = lax.axis_size("expert")
    capacity = min(tokens_here, tokens_here * top_count * 9 // (8 * experts))
    position, weight = slot_maps(routes, route_weights, experts)
    code = jnp.where(position >= 0, position + Place().member() * capacity, -1)
    meta = jnp.stack([code.astype(jnp.float32), weight])
    gate_up = expert_gate_up.reshape(expert_gate_up.shape[1], -1)
    teacher = experts_output(teacher_in, meta, gate_up, expert_down[0], capacity)
    return finish(teacher, student_in, norm_gain, projector, second_moment)


def solution(mesh):
    placed = (
        P("expert", None),
        P("expert", None),
        P("expert", None),
        P("expert", None, None, "fsdp"),
        P("expert", "fsdp", None),
        P("expert", None),
        P(),
        P(None, "fsdp"),
        P("expert", "fsdp"),
    )
    return jax.shard_map(
        per_device,
        mesh=mesh,
        in_specs=placed,
        out_specs=(P("expert", None), P("expert", "fsdp")),
        check_vma=False,
    )
```

```python
import functools
import types

import jax
import jax.numpy as jnp
from jax import lax
from jax.experimental import pallas as pl
from jax.experimental.pallas import tpu as pltpu
from jax.sharding import PartitionSpec as P

beta_two = 0.95
MESH = pl.DeviceIdType.MESH
NX, NZ, NY = 4, 8, 4
OCT = 2 * NX
WIDTH = 256
ORDER = (0, 4, 3, 5, 2, 6, 1, 7)


def remote(src, dst, send_sem, recv_sem, expert, share):
    return pltpu.make_async_remote_copy(
        src_ref=src,
        dst_ref=dst,
        send_sem=send_sem,
        recv_sem=recv_sem,
        device_id=(expert, share),
        device_id_type=MESH,
    )


class Place:
    def __init__(self):
        expert = lax.axis_index("expert")
        self.y = lax.axis_index("fsdp")
        self.x = expert // (2 * NZ)
        self.z = lax.rem(expert // 2, NZ)
        self.k = lax.rem(expert, 2)

    def at(self, dx=0, dz=0, dk=0):
        x = lax.rem(self.x + dx, NX)
        z = lax.rem(self.z + dz, NZ)
        k = lax.rem(self.k + dk, 2)
        return (x * NZ + z) * 2 + k

    def member(self, dx=0, dk=0):
        return lax.rem(self.x + dx, NX) * 2 + lax.rem(self.k + dk, 2)


def meet(place):
    barrier = pltpu.get_barrier_semaphore()
    peers = [(place.at(dx=dx, dk=dk), place.y) for dx in range(NX) for dk in range(2) if dx or dk]
    peers += [(place.at(dz=dz), place.y) for dz in range(1, NZ)]
    peers += [(place.at(), lax.rem(place.y + dy, NY)) for dy in range(1, NY)]
    for peer in peers:
        pl.semaphore_signal(barrier, inc=1, device_id=peer, device_id_type=MESH)
    pl.semaphore_wait(barrier, len(peers))


def cut_of(n, width):
    return slice(n * width, (n + 1) * width)


def part_of(index, size):
    return pl.ds(pl.multiple_of(index * size, size), size)


def norm(wide):
    inv = lax.rsqrt(jnp.mean(wide * wide, axis=1, keepdims=True) + 1e-06)
    return inv, wide * inv


def dot(a, b):
    return jnp.dot(a, b, preferred_element_type=jnp.float32)


class Gather:
    def __init__(self, place, send, landed, ref, tokens, width, sems):
        self.place, self.send, self.landed = place, send, landed
        self.ref, self.tokens, self.width = ref, tokens, width
        self.near_s, self.near_r, self.pass_s, self.pass_r = sems

    def slot(self, c, dx=0, dk=0):
        at = part_of(self.place.member(dx, dk), self.tokens)
        return self.ref.at[at, cut_of(c, self.width)]

    def start(self, c, own=None):
        own = self.slot(c) if own is None else own
        for i, dx, dk in ((1, 1, 0), (3, NX - 1, 0), (0, 0, 1)):
            to = self.place.at(dx=dx, dk=dk)
            self.send(own, self.slot(c), self.near_s.at[i, c], self.near_r.at[i, c], to, self.place.y)

    def onward(self, c, i):
        arrived = self.slot(c, NX - i)
        to = self.place.at(dk=1)
        self.send(arrived, arrived, self.pass_s.at[i - 1, c], self.pass_r.at[i - 1, c], to, self.place.y)

    def relay(self, c):
        for i in (1, 3):
            self.landed(self.slot(c, NX - i), self.near_s.at[i, c], self.near_r.at[i, c])
            if i == (1 if c % 2 == 0 else 3):
                arrived = self.slot(c, NX - i)
                to = self.place.at(dx=i)
                self.send(arrived, arrived, self.near_s.at[2, c], self.near_r.at[2, c], to, self.place.y)
            self.onward(c, i)

    def far(self, c):
        self.landed(self.slot(c, 2), self.near_s.at[2, c], self.near_r.at[2, c])
        self.onward(c, 2)

    def finish(self, c):
        self.landed(self.slot(c, 0, 1), self.near_s.at[0, c], self.near_r.at[0, c])
        for i in (1, 3, 2):
            self.landed(self.slot(c, NX - i, 1), self.pass_s.at[i - 1, c], self.pass_r.at[i - 1, c])


def layer_kernel(names, *refs):
    r = types.SimpleNamespace(**dict(zip(names, refs)))
    place = Place()
    y = place.y
    tokens, features = r.student.shape
    part = r.projector.shape[1]
    units = r.down.shape[0]
    block = r.rows.shape[2]
    piece = r.step.shape[0]
    share_rows = tokens // NY
    chunks = part // WIDTH
    f32, bf16 = jnp.float32, jnp.bfloat16
    mine = place.member()
    steps = len(ORDER)
    after, ahead = lax.rem(y + 1, NY), lax.rem(y + NY - 1, NY)

    own_tokens = r.tok.at[part_of(mine, tokens)]
    loads = [
        pltpu.make_async_copy(r.teacher_in.at[:, part_of(y, part)], own_tokens, r.load.at[0]),
        pltpu.make_async_copy(r.projector, r.proj, r.load.at[1]),
        pltpu.make_async_copy(r.gate_up, r.gates, r.load.at[2]),
        pltpu.make_async_copy(r.down.at[:, part_of(y, part)], r.down_all.at[0], r.load.at[3]),
    ]
    for load in loads:
        load.start()
    meet(place)
    sends = []

    def send(*args):
        copy = remote(*args)
        copy.start()
        sends.append(copy)

    def landed(ref, send_sem, recv_sem):
        remote(ref, ref, send_sem, recv_sem, place.at(), y).wait_recv()

    members = [(dx, dk) for dx in range(NX) for dk in range(2) if dx or dk]

    half = part // 2
    tok = Gather(
        place, send, landed, r.tok, tokens, half, (r.tok_s, r.tok_r, r.tokf_s, r.tokf_r)
    )
    for i, (dx, dk) in enumerate(members):
        to = place.at(dx=dx, dk=dk)
        send(r.meta.at[place.member(dx, dk)], r.metas.at[mine], r.meta_s.at[i], r.meta_r.at[i], to, y)
    loads[0].wait()
    for c in range(2):
        tok.start(c)
    for dy in (2, 1, 3):
        to = lax.rem(y + dy, NY)
        send(
            r.down.at[:, part_of(to, part)],
            r.down_all.at[dy],
            r.down_s.at[dy - 1],
            r.down_r.at[dy - 1],
            place.at(),
            to,
        )
    r.metas[mine] = r.meta[mine]
    for i, (dx, dk) in enumerate(members):
        landed(r.metas.at[place.member(NX - dx, dk)], r.meta_s.at[i], r.meta_r.at[i])
    for c in range(2):
        tok.relay(c)

    number = lax.broadcasted_iota(jnp.int32, (block, tokens), 0).astype(f32)
    for dk in (1, 0):
        for dx in range(NX):
            o = place.member(dx, dk)
            pieces = []
            for dz in range(NZ):
                at = pl.ds(lax.rem(place.z + dz, NZ), 1)
                pieces.append(jnp.where(number == r.metas[o, 0, at, :], r.metas[o, 1, at, :], 0.0))
            at = ((1 - dk) * NX + dx) * tokens
            r.spread[at : at + tokens, :] = jnp.concatenate(pieces, axis=0).T.astype(bf16)
    for c in range(2):
        tok.far(c)

    gain = r.gain[...]
    feat = norm(r.student[...].astype(f32))[1] * gain
    r.feat[...] = feat.astype(bf16)
    for x in range(NX):
        for z in range(NZ):
            for k in range(2):
                at = ((x * NZ + z) * 2 + k) * piece
                if at % tokens == 0:
                    turned = feat[:, at : at + tokens].T.astype(bf16)
                r.slab[x * 2 + k, z * piece : (z + 1) * piece, :] = turned[
                    at % tokens : at % tokens + piece
                ]
    for c in range(2):
        tok.finish(c)

    for dz in ORDER:
        at = pl.ds(lax.rem(place.z + dz, NZ), 1)
        for o in range(OCT):
            r.select[:, cut_of(o, tokens)] = jnp.where(number == r.metas[o, 0, at, :], 1.0, 0.0).astype(
                bf16
            )
        picked = dot(r.select[...], r.tok[...]).astype(bf16)
        if dz == 0:
            r.rows[0, 0] = picked
            send(r.rows.at[0, 0], r.rows.at[1, 0], r.up_s.at[0], r.up_r.at[0], place.at(), after)
            send(r.rows.at[0, 0], r.rows.at[3, 0], r.low_s.at[0], r.low_r.at[0], place.at(), ahead)
        else:
            r.out[dz - 1] = picked
            send(
                r.out.at[dz - 1], r.rows.at[0, dz], r.z_s.at[dz - 1], r.z_r.at[dz - 1], place.at(dz=dz), y
            )

    slot = part_of(mine, tokens)
    for i, (dx, dk) in enumerate(members):
        send(
            r.slab.at[place.member(dx, dk)],
            r.slabs.at[:, slot],
            r.slab_s.at[i],
            r.slab_r.at[i],
            place.at(dx=dx, dk=dk),
            y,
        )
    r.slabs[:, slot] = r.slab[mine]
    loads[1].wait()
    loads[2].wait()
    loads[3].wait()

    def pass_rows(j):
        dz = ORDER[j]
        landed(r.rows.at[0, dz], r.z_s.at[dz - 1], r.z_r.at[dz - 1])
        send(r.rows.at[0, dz], r.rows.at[1, dz], r.up_s.at[dz], r.up_r.at[dz], place.at(), after)
        send(r.rows.at[0, dz], r.rows.at[3, dz], r.low_s.at[dz], r.low_r.at[dz], place.at(), ahead)

    def relay_rows(j):
        dz = ORDER[j]
        landed(r.rows.at[1, dz], r.up_s.at[dz], r.up_r.at[dz])
        landed(r.rows.at[3, dz], r.low_s.at[dz], r.low_r.at[dz])
        source, to = (1, after) if j % 2 == 0 else (3, ahead)
        send(r.rows.at[source, dz], r.rows.at[2, dz], r.far_s.at[dz], r.far_r.at[dz], place.at(), to)

    def first_product(j):
        dz = ORDER[j]
        landed(r.rows.at[2, dz], r.far_s.at[dz], r.far_r.at[dz])
        out = jnp.zeros((block, 2 * units), f32)
        for ry in range(NY):
            share = lax.rem(y + NY - ry, NY)
            out += dot(r.rows[ry, dz], r.gates[part_of(share, part), :])
        gate, up = out[:, :units], out[:, units:]
        r.hidden[0, dz] = (gate / (1.0 + jnp.exp(-gate)) * up).astype(bf16)
        for dy, to in ((1, after), (3, ahead)):
            send(
                r.hidden.at[0, dz], r.hidden.at[dy, dz], r.hid_s.at[dy, dz], r.hid_r.at[dy, dz], place.at(), to
            )

    def relay_hidden(j):
        dz = ORDER[j]
        for dy in (1, 3):
            landed(r.hidden.at[dy, dz], r.hid_s.at[dy, dz], r.hid_r.at[dy, dz])
        source, to = (1, after) if j % 2 == 0 else (3, ahead)
        send(r.hidden.at[source, dz], r.hidden.at[2, dz], r.hid_s.at[2, dz], r.hid_r.at[2, dz], place.at(), to)

    def second_product(j):
        dz = ORDER[j]
        landed(r.hidden.at[2, dz], r.hid_s.at[2, dz], r.hid_r.at[2, dz])
        out = jnp.zeros((block, part), f32)
        for ry in range(NY):
            out += dot(r.hidden[ry, dz], r.down_all[ry])
        if dz == 0:
            r.home[0:block, :] = out.astype(bf16)
        else:
            r.back[dz - 1] = out.astype(bf16)
            send(
                r.back.at[dz - 1],
                r.home.at[cut_of(dz, block)],
                r.ret_s.at[dz - 1],
                r.ret_r.at[dz - 1],
                place.at(dz=NZ - dz),
                y,
            )

    for j in range(1, steps + 4):
        if j < steps:
            pass_rows(j)
        if 0 <= j - 1 < steps:
            relay_rows(j - 1)
        if j == 1:
            for n in range(chunks):
                r.dense[:, cut_of(n, WIDTH)] = dot(r.feat[...], r.proj[:, cut_of(n, WIDTH)])
        if 0 <= j - 2 < steps:
            first_product(j - 2)
        if 0 <= j - 3 < steps:
            relay_hidden(j - 3)
        if j == 4:
            for dy in range(1, NY):
                landed(r.down_all.at[dy], r.down_s.at[dy - 1], r.down_r.at[dy - 1])
        if 0 <= j - 4 < steps:
            second_product(j - 4)

    for dz in ORDER[1:]:
        landed(r.home.at[cut_of(dz, block)], r.ret_s.at[dz - 1], r.ret_r.at[dz - 1])

    count = NX * tokens
    for n in range(chunks):
        r.half[n] = dot(r.spread[:count, :], r.home[:, cut_of(n, WIDTH)]).astype(bf16)
        send(r.half.at[n], r.half_in.at[n], r.half_s.at[n], r.half_r.at[n], place.at(dk=1), y)
    for n in range(chunks):
        r.total[n] = dot(r.spread[count:, :], r.home[:, cut_of(n, WIDTH)])
        landed(r.half_in.at[n], r.half_s.at[n], r.half_r.at[n])
        for dx in (2, 1, 3):
            at = cut_of(dx, tokens)
            r.third[dx - 1, n] = (r.total[n, at, :] + r.half_in[n, at, :].astype(f32)).astype(bf16)
            send(
                r.third.at[dx - 1, n],
                r.third_in.at[dx - 1, n],
                r.third_s.at[dx - 1, n],
                r.third_r.at[dx - 1, n],
                place.at(dx=dx),
                y,
            )

    res = Gather(
        place, send, landed, r.residue, tokens, WIDTH, (r.res_s, r.res_r, r.resf_s, r.resf_r)
    )
    for n in range(chunks + 2):
        if n < chunks:
            teacher = r.total[n, :tokens, :] + r.half_in[n, :tokens, :].astype(f32)
            for dx in (1, 3, 2):
                landed(r.third_in.at[dx - 1, n], r.third_s.at[dx - 1, n], r.third_r.at[dx - 1, n])
                teacher += r.third_in[dx - 1, n].astype(f32)
            cut = cut_of(n, WIDTH)
            r.residue[slot, cut] = (r.dense[:, cut] - teacher).astype(bf16)
            res.start(n)
        if 0 <= n - 1 < chunks:
            res.relay(n - 1)
        if 0 <= n - 2 < chunks:
            res.far(n - 2)

    for n in range(features // WIDTH):
        r.part[:, cut_of(n, WIDTH)] = lax.dot_general(
            r.residue[slot, :],
            r.proj[cut_of(n, WIDTH), :],
            (((1,), (1,)), ((), ())),
            preferred_element_type=f32,
        ).astype(bf16)
    for dy in (2, 1, 3):
        to = lax.rem(y + dy, NY)
        send(
            r.part.at[part_of(to, share_rows)],
            r.parts.at[dy - 1],
            r.part_s.at[dy - 1],
            r.part_r.at[dy - 1],
            place.at(),
            to,
        )

    for i, (dx, dk) in enumerate(members):
        at = part_of(place.member(NX - dx, dk), tokens)
        landed(r.slabs.at[:, at], r.slab_s.at[i], r.slab_r.at[i])
    for n in range(chunks):
        res.finish(n)
        grad = dot(r.slabs[...], r.residue[:, cut_of(n, WIDTH)]).reshape(NZ, piece, WIDTH)
        r.grad[n] = grad.astype(bf16)
        r.own_grad[n] = grad
        for dz in (4, 3, 5, 2, 6, 1, 7):
            send(
                r.grad.at[n, lax.rem(place.z + dz, NZ)],
                r.grads.at[dz - 1, n],
                r.grad_s.at[dz - 1, n],
                r.grad_r.at[dz - 1, n],
                place.at(dz=dz),
                y,
            )

    own_rows = part_of(y, share_rows)
    feat_grad = r.part[own_rows, :].astype(f32)
    for dy in range(1, NY):
        landed(r.parts.at[dy - 1], r.part_s.at[dy - 1], r.part_r.at[dy - 1])
        feat_grad += r.parts[dy - 1].astype(f32)
    inv, normed = norm(r.student[own_rows, :].astype(f32))
    scaled = feat_grad * gain
    r.d_own[...] = (
        inv * (scaled - normed * jnp.mean(scaled * normed, axis=1, keepdims=True))
    ).astype(bf16)
    for dy in (2, 1, 3):
        to = lax.rem(y + dy, NY)
        send(r.d_own, r.d_all.at[dy - 1], r.d_s.at[dy - 1], r.d_r.at[dy - 1], place.at(), to)
    r.d[own_rows, :] = r.d_own[...]

    for n in range(chunks):
        total = r.own_grad[n, place.z]
        for dz in (1, 7, 2, 6, 3, 5, 4):
            landed(r.grads.at[dz - 1, n], r.grad_s.at[dz - 1, n], r.grad_r.at[dz - 1, n])
            total += r.grads[dz - 1, n].astype(f32)
        cut = cut_of(n, WIDTH)
        r.step[:, cut] = total * lax.rsqrt(
            beta_two * r.moment[:, cut] + (1.0 - beta_two) * total * total
        )
    for dy in range(1, NY):
        landed(r.d_all.at[dy - 1], r.d_s.at[dy - 1], r.d_r.at[dy - 1])
        r.d[part_of(lax.rem(y + NY - dy, NY), share_rows), :] = r.d_all[dy - 1]
    for copy in sends:
        copy.wait_send()


def layer(teacher_in, meta, gate_up, down, student_in, norm_gain, projector, second_moment, capacity):
    tokens, features = student_in.shape
    part = projector.shape[1]
    units = down.shape[0]
    block = OCT * capacity
    piece = second_moment.shape[0]
    share_rows = tokens // NY
    chunks = part // WIDTH
    bf16, f32 = jnp.bfloat16, jnp.float32
    vmem, anywhere = pl.BlockSpec(memory_space=pltpu.VMEM), pl.BlockSpec(memory_space=pl.ANY)
    inputs = dict(
        teacher_in=(teacher_in, anywhere),
        meta=(meta, vmem),
        gate_up=(gate_up, anywhere),
        down=(down, anywhere),
        student=(student_in, vmem),
        gain=(norm_gain.reshape(1, -1), vmem),
        projector=(projector, anywhere),
        moment=(second_moment, vmem),
    )
    outputs = dict(
        d=jax.ShapeDtypeStruct((tokens, features), bf16),
        step=jax.ShapeDtypeStruct(second_moment.shape, f32),
    )
    buffers = dict(
        proj=(projector.shape, bf16),
        gates=(gate_up.shape, bf16),
        tok=((OCT * tokens, part), bf16),
        metas=(meta.shape, f32),
        select=((block, OCT * tokens), bf16),
        spread=((OCT * tokens, NZ * block), bf16),
        out=((NZ - 1, block, part), bf16),
        rows=((NY, NZ, block, part), bf16),
        hidden=((NY, NZ, block, units), bf16),
        down_all=((NY, units, part), bf16),
        back=((NZ - 1, block, part), bf16),
        home=((NZ * block, part), bf16),
        half=((chunks, NX * tokens, WIDTH), bf16),
        half_in=((chunks, NX * tokens, WIDTH), bf16),
        total=((chunks, NX * tokens, WIDTH), f32),
        third=((NX - 1, chunks, tokens, WIDTH), bf16),
        third_in=((NX - 1, chunks, tokens, WIDTH), bf16),
        feat=((tokens, features), bf16),
        dense=((tokens, part), f32),
        slab=((OCT, NZ * piece, tokens), bf16),
        slabs=((NZ * piece, OCT * tokens), bf16),
        residue=((OCT * tokens, part), bf16),
        part=((tokens, features), bf16),
        parts=((NY - 1, share_rows, features), bf16),
        d_own=((share_rows, features), bf16),
        d_all=((NY - 1, share_rows, features), bf16),
        grad=((chunks, NZ, piece, WIDTH), bf16),
        grads=((NZ - 1, chunks, piece, WIDTH), bf16),
        own_grad=((chunks, NZ, piece, WIDTH), f32),
    )
    flights = dict(
        meta=(OCT - 1,),
        tok=(4, 2),
        tokf=(3, 2),
        down=(NY - 1,),
        z=(NZ - 1,),
        up=(NZ,),
        low=(NZ,),
        far=(NZ,),
        hid=(NY, NZ),
        ret=(NZ - 1,),
        half=(chunks,),
        third=(NX - 1, chunks),
        slab=(OCT - 1,),
        res=(4, chunks),
        resf=(3, chunks),
        part=(NY - 1,),
        d=(NY - 1,),
        grad=(NZ - 1, chunks),
    )
    dma = pltpu.SemaphoreType.DMA
    pairs = {f"{name}_{end}": dma(shape) for name, shape in flights.items() for end in "sr"}
    names = (*inputs, *outputs, *buffers, *pairs, "load")
    return pl.pallas_call(
        functools.partial(layer_kernel, names),
        out_shape=tuple(outputs.values()),
        in_specs=[spec for _, spec in inputs.values()],
        out_specs=[vmem] * len(outputs),
        scratch_shapes=[pltpu.VMEM(*b) for b in buffers.values()] + [*pairs.values(), dma((4,))],
        compiler_params=pltpu.CompilerParams(
            collective_id=0, has_side_effects=True, vmem_limit_bytes=60 << 20
        ),
    )(*(value for value, _ in inputs.values()))


def slot_maps(routes, route_weights, experts):
    tokens = routes.shape[0]
    named = routes[:, :, None] == jnp.arange(experts, dtype=jnp.int32)[None, None, :]
    member = jnp.any(named, axis=1)
    weight = jnp.sum(jnp.where(named, route_weights[:, :, None], 0.0), axis=1)
    earlier = jnp.tril(jnp.ones((tokens, tokens), jnp.bfloat16), -1)
    before = jnp.dot(earlier, member.astype(jnp.bfloat16), preferred_element_type=jnp.float32)
    position = jnp.where(member, before.astype(jnp.int32), -1)
    return position.T, weight.T


def per_device(
    teacher_in,
    routes,
    route_weights,
    expert_gate_up,
    expert_down,
    student_in,
    norm_gain,
    projector,
    second_moment,
):
    tokens_here = teacher_in.shape[0]
    top_count = routes.shape[1]
    experts = lax.axis_size("expert")
    capacity = min(tokens_here, tokens_here * top_count * 9 // (8 * experts))
    position, weight = slot_maps(routes, route_weights, experts)
    code = jnp.where(position >= 0, position + Place().member() * capacity, -1)
    meta = jnp.stack([code.astype(jnp.float32), weight])
    meta = meta.reshape(2, NX, NZ, 2, tokens_here).transpose(1, 3, 0, 2, 4)
    meta = meta.reshape(OCT, 2, NZ, tokens_here)
    gate_up = expert_gate_up.reshape(expert_gate_up.shape[1], -1)
    return layer(
        teacher_in,
        meta,
        gate_up,
        expert_down[0],
        student_in,
        norm_gain,
        projector,
        second_moment,
        capacity,
    )


def solution(mesh):
    placed = (
        P("expert", None),
        P("expert", None),
        P("expert", None),
        P("expert", None, None, "fsdp"),
        P("expert", "fsdp", None),
        P("expert", None),
        P(),
        P(None, "fsdp"),
        P("expert", "fsdp"),
    )
    return jax.shard_map(
        per_device,
        mesh=mesh,
        in_specs=placed,
        out_specs=(P("expert", None), P("expert", "fsdp")),
        check_vma=False,
    )
```

```python
import functools
import types

import jax
import jax.numpy as jnp
from jax import lax
from jax.experimental import pallas as pl
from jax.experimental.pallas import tpu as pltpu
from jax.sharding import PartitionSpec as P

beta_two = 0.95
MESH = pl.DeviceIdType.MESH
NX, NZ, NY = 4, 8, 4
OCT = 2 * NX
WIDTH = 256
ORDER = (0, 1, 2, 6, 4, 5, 3, 7)


def remote(src, dst, send_sem, recv_sem, expert, share):
    return pltpu.make_async_remote_copy(
        src_ref=src,
        dst_ref=dst,
        send_sem=send_sem,
        recv_sem=recv_sem,
        device_id=(expert, share),
        device_id_type=MESH,
    )


class Place:
    def __init__(self):
        expert = lax.axis_index("expert")
        self.y = lax.axis_index("fsdp")
        self.x = expert // (2 * NZ)
        self.z = lax.rem(expert // 2, NZ)
        self.k = lax.rem(expert, 2)

    def at(self, dx=0, dz=0, dk=0):
        x = lax.rem(self.x + dx, NX)
        z = lax.rem(self.z + dz, NZ)
        k = lax.rem(self.k + dk, 2)
        return (x * NZ + z) * 2 + k

    def member(self, dx=0, dk=0):
        return lax.rem(self.x + dx, NX) * 2 + lax.rem(self.k + dk, 2)


def meet(place):
    barrier = pltpu.get_barrier_semaphore()
    peers = [(place.at(dx=dx, dk=dk), place.y) for dx in range(NX) for dk in range(2) if dx or dk]
    peers += [(place.at(dz=dz), place.y) for dz in range(1, NZ)]
    peers += [(place.at(), lax.rem(place.y + dy, NY)) for dy in range(1, NY)]
    for peer in peers:
        pl.semaphore_signal(barrier, inc=1, device_id=peer, device_id_type=MESH)
    pl.semaphore_wait(barrier, len(peers))


def cut_of(n, width):
    return slice(n * width, (n + 1) * width)


def part_of(index, size):
    return pl.ds(pl.multiple_of(index * size, size), size)


def norm(wide):
    inv = lax.rsqrt(jnp.mean(wide * wide, axis=1, keepdims=True) + 1e-06)
    return inv, wide * inv


def dot(a, b):
    return jnp.dot(a, b, preferred_element_type=jnp.float32)


class Gather:
    def __init__(self, place, send, landed, ref, tokens, width, sems):
        self.place, self.send, self.landed = place, send, landed
        self.ref, self.tokens, self.width = ref, tokens, width
        self.near_s, self.near_r, self.pass_s, self.pass_r = sems

    def slot(self, c, dx=0, dk=0):
        at = part_of(self.place.member(dx, dk), self.tokens)
        return self.ref.at[at, cut_of(c, self.width)]

    def start(self, c, own=None):
        own = self.slot(c) if own is None else own
        for i, dx, dk in ((1, 1, 0), (3, NX - 1, 0), (0, 0, 1)):
            to = self.place.at(dx=dx, dk=dk)
            self.send(own, self.slot(c), self.near_s.at[i, c], self.near_r.at[i, c], to, self.place.y)

    def onward(self, c, i):
        arrived = self.slot(c, NX - i)
        to = self.place.at(dk=1)
        self.send(arrived, arrived, self.pass_s.at[i - 1, c], self.pass_r.at[i - 1, c], to, self.place.y)

    def relay(self, c):
        for i in (1, 3):
            self.landed(self.slot(c, NX - i), self.near_s.at[i, c], self.near_r.at[i, c])
            if i == (1 if c % 2 == 0 else 3):
                arrived = self.slot(c, NX - i)
                to = self.place.at(dx=i)
                self.send(arrived, arrived, self.near_s.at[2, c], self.near_r.at[2, c], to, self.place.y)
            self.onward(c, i)

    def far(self, c):
        self.landed(self.slot(c, 2), self.near_s.at[2, c], self.near_r.at[2, c])
        self.onward(c, 2)

    def finish(self, c):
        self.landed(self.slot(c, 0, 1), self.near_s.at[0, c], self.near_r.at[0, c])
        for i in (1, 3, 2):
            self.landed(self.slot(c, NX - i, 1), self.pass_s.at[i - 1, c], self.pass_r.at[i - 1, c])


def layer_kernel(names, *refs):
    r = types.SimpleNamespace(**dict(zip(names, refs)))
    place = Place()
    y = place.y
    tokens, features = r.student.shape
    part = r.projector.shape[1]
    units = r.down.shape[0]
    block = r.rows.shape[2]
    piece = r.step.shape[0]
    share_rows = tokens // NY
    chunks = part // WIDTH
    f32, bf16 = jnp.float32, jnp.bfloat16
    mine = place.member()
    steps = len(ORDER)
    after, ahead = lax.rem(y + 1, NY), lax.rem(y + NY - 1, NY)

    capacity = block // NZ
    far_share = lax.rem(y + 2, NY)
    loads = [
        pltpu.make_async_copy(
            r.teacher_in.at[:, part_of(y, part)], r.tok.at[0, cut_of(0, tokens)], r.load.at[0]
        ),
        pltpu.make_async_copy(
            r.teacher_in.at[:, part_of(far_share, part)], r.tok.at[1, cut_of(0, tokens)], r.load.at[1]
        ),
        pltpu.make_async_copy(r.projector, r.proj, r.load.at[2]),
        pltpu.make_async_copy(r.gate_up, r.gates, r.load.at[3]),
        pltpu.make_async_copy(r.down.at[:, part_of(y, part)], r.down_all.at[0], r.load.at[4]),
    ]
    for load in loads:
        load.start()
    meet(place)
    sends = []

    def send(*args):
        copy = remote(*args)
        copy.start()
        sends.append(copy)

    def landed(ref, send_sem, recv_sem):
        remote(ref, ref, send_sem, recv_sem, place.at(), y).wait_recv()

    members = [(dx, dk) for dx in range(NX) for dk in range(2) if dx or dk]

    half = part // 2

    def ring_slot(q, way, hops, c):
        d = hops if way == 0 else (NZ - hops) % NZ
        return r.tok.at[q, cut_of(d, tokens), cut_of(c, half)]

    def ring_send(q, way, hops, c):
        i = way * NZ + hops * 2 + c
        send(
            ring_slot(q, way, hops, c),
            ring_slot(q, way, hops + 1, c),
            r.tok_s.at[q, i],
            r.tok_r.at[q, i],
            place.at(dz=1 if way == 0 else NZ - 1),
            y,
        )

    def ring_start(q):
        for c in range(2):
            for way in range(2):
                ring_send(q, way, 0, c)

    def ring_step(q, hops):
        for c in range(2):
            for way in range(2):
                if hops < NZ // 2 or c == way:
                    i = way * NZ + (hops - 1) * 2 + c
                    landed(ring_slot(q, way, hops, c), r.tok_s.at[q, i], r.tok_r.at[q, i])
                if hops < NZ // 2 - 1 or (hops == NZ // 2 - 1 and c == way):
                    ring_send(q, way, hops, c)

    for dz in range(1, NZ):
        send(
            r.meta.at[lax.rem(place.z + dz, NZ)],
            r.metas.at[dz],
            r.meta_s.at[dz - 1],
            r.meta_r.at[dz - 1],
            place.at(dz=dz),
            y,
        )
    loads[0].wait()
    ring_start(0)
    for dy in (2, 1, 3):
        to = lax.rem(y + dy, NY)
        send(
            r.down.at[:, part_of(to, part)],
            r.down_all.at[dy],
            r.down_s.at[dy - 1],
            r.down_r.at[dy - 1],
            place.at(),
            to,
        )
    r.metas[0] = r.meta[place.z]
    ring_step(0, 1)

    gain = r.gain[...]
    feat = norm(r.student[...].astype(f32))[1] * gain
    r.feat[...] = feat.astype(bf16)
    ring_step(0, 2)

    for x in range(NX):
        for z in range(NZ):
            for k in range(2):
                at = ((x * NZ + z) * 2 + k) * piece
                if at % tokens == 0:
                    turned = feat[:, at : at + tokens].T.astype(bf16)
                r.slab[x * 2 + k, z * piece : (z + 1) * piece, :] = turned[
                    at % tokens : at % tokens + piece
                ]
    ring_step(0, 3)
    loads[1].wait()
    ring_start(1)
    for dz in range(1, NZ):
        landed(r.metas.at[dz], r.meta_s.at[dz - 1], r.meta_r.at[dz - 1])
    ring_step(0, 4)

    number = lax.broadcasted_iota(jnp.int32, (block, tokens), 0).astype(f32)

    def expert_at(i):
        return pl.ds(place.member(i // 2, i % 2), 1)

    def select_rows(q, i):
        for d in range(NZ):
            code = r.metas[d, 0, expert_at(i), :] + float(d * capacity)
            r.select[:, cut_of(d, tokens)] = jnp.where(number == code, 1.0, 0.0).astype(bf16)
        picked = dot(r.select[...], r.tok[q]).astype(bf16)
        if i == 0:
            r.rows[2 * q, 0] = picked
        else:
            r.out[q, i - 1] = picked
            send(
                r.out.at[q, i - 1],
                r.rows.at[2 * q, i],
                r.x_s.at[q, i - 1],
                r.x_r.at[q, i - 1],
                place.at(dx=i // 2, dk=i % 2),
                y,
            )

    def pass_rows(j):
        i = ORDER[j]
        if i:
            landed(r.rows.at[0, i], r.x_s.at[0, i - 1], r.x_r.at[0, i - 1])
        send(r.rows.at[0, i], r.rows.at[1, i], r.up_s.at[i], r.up_r.at[i], place.at(), after)
        send(r.rows.at[0, i], r.rows.at[3, i], r.low_s.at[i], r.low_r.at[i], place.at(), ahead)

    for j in range(steps):
        select_rows(0, ORDER[j])
        if j == 0:
            pass_rows(0)
        if j % 2 == 1:
            ring_step(1, (j + 1) // 2)
        if j >= 3:
            pass_rows(j - 2)
    for j in range(steps):
        select_rows(1, ORDER[j])
        if j < 2:
            pass_rows(steps - 2 + j)

    slot = part_of(mine, tokens)
    for i, (dx, dk) in enumerate(members):
        send(
            r.slab.at[place.member(dx, dk)],
            r.slabs.at[:, slot],
            r.slab_s.at[i],
            r.slab_r.at[i],
            place.at(dx=dx, dk=dk),
            y,
        )
    r.slabs[:, slot] = r.slab[mine]
    for load in loads[2:]:
        load.wait()

    def first_product(j):
        i = ORDER[j]
        if i:
            landed(r.rows.at[2, i], r.x_s.at[1, i - 1], r.x_r.at[1, i - 1])
        landed(r.rows.at[1, i], r.up_s.at[i], r.up_r.at[i])
        landed(r.rows.at[3, i], r.low_s.at[i], r.low_r.at[i])
        out = jnp.zeros((block, 2 * units), f32)
        for ry in range(NY):
            share = lax.rem(y + NY - ry, NY)
            out += dot(r.rows[ry, i], r.gates[part_of(share, part), :])
        gate, up = out[:, :units], out[:, units:]
        r.hidden[0, i] = (gate / (1.0 + jnp.exp(-gate)) * up).astype(bf16)
        for dy, to in ((1, after), (3, ahead)):
            send(
                r.hidden.at[0, i], r.hidden.at[dy, i], r.hid_s.at[dy, i], r.hid_r.at[dy, i], place.at(), to
            )

    def relay_hidden(j):
        i = ORDER[j]
        for dy in (1, 3):
            landed(r.hidden.at[dy, i], r.hid_s.at[dy, i], r.hid_r.at[dy, i])
        source, to = (1, after) if j % 2 == 0 else (3, ahead)
        send(r.hidden.at[source, i], r.hidden.at[2, i], r.hid_s.at[2, i], r.hid_r.at[2, i], place.at(), to)

    def second_product(j):
        i = ORDER[j]
        landed(r.hidden.at[2, i], r.hid_s.at[2, i], r.hid_r.at[2, i])
        out = jnp.zeros((block, part), f32)
        for ry in range(NY):
            out += dot(r.hidden[ry, i], r.down_all[ry])
        if i == 0:
            r.home[0:block, :] = out.astype(bf16)
        else:
            r.back[i - 1] = out.astype(bf16)
            send(
                r.back.at[i - 1],
                r.home.at[cut_of(i, block)],
                r.ret_s.at[i - 1],
                r.ret_r.at[i - 1],
                place.at(dx=NX - i // 2, dk=i % 2),
                y,
            )

    def weigh(d):
        pieces = []
        for i in range(OCT):
            code = r.metas[d, 0, expert_at(i), :] + float(d * capacity)
            pieces.append(jnp.where(number == code, r.metas[d, 1, expert_at(i), :], 0.0))
        r.spread[cut_of(d, tokens), :] = jnp.concatenate(pieces, axis=0).T.astype(bf16)

    for j in range(steps + 2):
        if j < steps:
            first_product(j)
        if 0 <= j - 1 < steps:
            relay_hidden(j - 1)
        if j == 1:
            for n in range(chunks):
                r.dense[:, cut_of(n, WIDTH)] = dot(r.feat[...], r.proj[:, cut_of(n, WIDTH)])
        if j == 2:
            for dy in range(1, NY):
                landed(r.down_all.at[dy], r.down_s.at[dy - 1], r.down_r.at[dy - 1])
        if 0 <= j - 2 < steps:
            second_product(j - 2)
        if j < steps:
            weigh(j)

    for i in range(1, OCT):
        landed(r.home.at[cut_of(i, block)], r.ret_s.at[i - 1], r.ret_r.at[i - 1])

    def sum_hop(n, way, left):
        d = left if way == 0 else NZ - left
        here = r.total[n, cut_of(d, tokens), :]
        if left < NZ // 2 - 1 or (left == NZ // 2 - 1 and n % 2 == way):
            i = left * chunks + n
            landed(r.sum_in.at[way, left, n], r.sum_s.at[way, i], r.sum_r.at[way, i])
            here += r.sum_in[way, left, n].astype(f32)
        r.sum_out[way, left - 1, n] = here.astype(bf16)
        i = (left - 1) * chunks + n
        send(
            r.sum_out.at[way, left - 1, n],
            r.sum_in.at[way, left - 1, n],
            r.sum_s.at[way, i],
            r.sum_r.at[way, i],
            place.at(dz=NZ - 1 if way == 0 else 1),
            y,
        )

    res = Gather(
        place, send, landed, r.residue, tokens, WIDTH, (r.res_s, r.res_r, r.resf_s, r.resf_r)
    )
    for wave in range(chunks + NZ // 2 + 2):
        if wave < chunks:
            r.total[wave] = dot(r.spread[...], r.home[:, cut_of(wave, WIDTH)])
        for n in range(chunks):
            hop = wave - n
            left = NZ // 2 - hop
            if hop == 0:
                sum_hop(n, n % 2, left)
            elif 0 < hop < NZ // 2:
                sum_hop(n, 0, left)
                sum_hop(n, 1, left)
            elif hop == NZ // 2:
                teacher = r.total[n, :tokens, :]
                for way in range(2):
                    landed(r.sum_in.at[way, 0, n], r.sum_s.at[way, n], r.sum_r.at[way, n])
                    teacher += r.sum_in[way, 0, n].astype(f32)
                cut = cut_of(n, WIDTH)
                r.residue[slot, cut] = (r.dense[:, cut] - teacher).astype(bf16)
                res.start(n)
            elif hop == NZ // 2 + 1:
                res.relay(n)
            elif hop == NZ // 2 + 2:
                res.far(n)
    for n in range(features // WIDTH):
        r.part[:, cut_of(n, WIDTH)] = lax.dot_general(
            r.residue[slot, :],
            r.proj[cut_of(n, WIDTH), :],
            (((1,), (1,)), ((), ())),
            preferred_element_type=f32,
        ).astype(bf16)
    for dy in (2, 1, 3):
        to = lax.rem(y + dy, NY)
        send(
            r.part.at[part_of(to, share_rows)],
            r.parts.at[dy - 1],
            r.part_s.at[dy - 1],
            r.part_r.at[dy - 1],
            place.at(),
            to,
        )

    for i, (dx, dk) in enumerate(members):
        at = part_of(place.member(NX - dx, dk), tokens)
        landed(r.slabs.at[:, at], r.slab_s.at[i], r.slab_r.at[i])
    for n in range(chunks):
        res.finish(n)
        grad = dot(r.slabs[...], r.residue[:, cut_of(n, WIDTH)]).reshape(NZ, piece, WIDTH)
        r.grad[n] = grad.astype(bf16)
        r.own_grad[n] = grad
        for dz in (4, 3, 5, 2, 6, 1, 7):
            send(
                r.grad.at[n, lax.rem(place.z + dz, NZ)],
                r.grads.at[dz - 1, n],
                r.grad_s.at[dz - 1, n],
                r.grad_r.at[dz - 1, n],
                place.at(dz=dz),
                y,
            )

    own_rows = part_of(y, share_rows)
    feat_grad = r.part[own_rows, :].astype(f32)
    for dy in range(1, NY):
        landed(r.parts.at[dy - 1], r.part_s.at[dy - 1], r.part_r.at[dy - 1])
        feat_grad += r.parts[dy - 1].astype(f32)
    inv, normed = norm(r.student[own_rows, :].astype(f32))
    scaled = feat_grad * gain
    r.d_own[...] = (
        inv * (scaled - normed * jnp.mean(scaled * normed, axis=1, keepdims=True))
    ).astype(bf16)
    for dy in (2, 1, 3):
        to = lax.rem(y + dy, NY)
        send(r.d_own, r.d_all.at[dy - 1], r.d_s.at[dy - 1], r.d_r.at[dy - 1], place.at(), to)
    r.d[own_rows, :] = r.d_own[...]

    for n in range(chunks):
        total = r.own_grad[n, place.z]
        for dz in (1, 7, 2, 6, 3, 5, 4):
            landed(r.grads.at[dz - 1, n], r.grad_s.at[dz - 1, n], r.grad_r.at[dz - 1, n])
            total += r.grads[dz - 1, n].astype(f32)
        cut = cut_of(n, WIDTH)
        r.step[:, cut] = total * lax.rsqrt(
            beta_two * r.moment[:, cut] + (1.0 - beta_two) * total * total
        )
    for dy in range(1, NY):
        landed(r.d_all.at[dy - 1], r.d_s.at[dy - 1], r.d_r.at[dy - 1])
        r.d[part_of(lax.rem(y + NY - dy, NY), share_rows), :] = r.d_all[dy - 1]
    for copy in sends:
        copy.wait_send()


def layer(teacher_in, meta, gate_up, down, student_in, norm_gain, projector, second_moment, capacity):
    tokens, features = student_in.shape
    part = projector.shape[1]
    units = down.shape[0]
    block = OCT * capacity
    piece = second_moment.shape[0]
    share_rows = tokens // NY
    chunks = part // WIDTH
    bf16, f32 = jnp.bfloat16, jnp.float32
    vmem, anywhere = pl.BlockSpec(memory_space=pltpu.VMEM), pl.BlockSpec(memory_space=pl.ANY)
    inputs = dict(
        teacher_in=(teacher_in, anywhere),
        meta=(meta, vmem),
        gate_up=(gate_up, anywhere),
        down=(down, anywhere),
        student=(student_in, vmem),
        gain=(norm_gain.reshape(1, -1), vmem),
        projector=(projector, anywhere),
        moment=(second_moment, vmem),
    )
    outputs = dict(
        d=jax.ShapeDtypeStruct((tokens, features), bf16),
        step=jax.ShapeDtypeStruct(second_moment.shape, f32),
    )
    buffers = dict(
        proj=(projector.shape, bf16),
        gates=(gate_up.shape, bf16),
        tok=((2, NZ * tokens, part), bf16),
        metas=(meta.shape, f32),
        select=((block, OCT * tokens), bf16),
        spread=((OCT * tokens, NZ * block), bf16),
        out=((2, OCT - 1, block, part), bf16),
        rows=((NY, NZ, block, part), bf16),
        hidden=((NY, NZ, block, units), bf16),
        down_all=((NY, units, part), bf16),
        back=((NZ - 1, block, part), bf16),
        home=((NZ * block, part), bf16),
        total=((chunks, NZ * tokens, WIDTH), f32),
        sum_out=((2, NZ // 2, chunks, tokens, WIDTH), bf16),
        sum_in=((2, NZ // 2, chunks, tokens, WIDTH), bf16),
        feat=((tokens, features), bf16),
        dense=((tokens, part), f32),
        slab=((OCT, NZ * piece, tokens), bf16),
        slabs=((NZ * piece, OCT * tokens), bf16),
        residue=((OCT * tokens, part), bf16),
        part=((tokens, features), bf16),
        parts=((NY - 1, share_rows, features), bf16),
        d_own=((share_rows, features), bf16),
        d_all=((NY - 1, share_rows, features), bf16),
        grad=((chunks, NZ, piece, WIDTH), bf16),
        grads=((NZ - 1, chunks, piece, WIDTH), bf16),
        own_grad=((chunks, NZ, piece, WIDTH), f32),
    )
    flights = dict(
        meta=(NZ - 1,),
        tok=(2, 2 * NZ),
        down=(NY - 1,),
        x=(2, OCT - 1),
        up=(OCT,),
        low=(OCT,),
        hid=(NY, OCT),
        ret=(OCT - 1,),
        sum=(2, NZ // 2 * chunks),
        slab=(OCT - 1,),
        res=(4, chunks),
        resf=(3, chunks),
        part=(NY - 1,),
        d=(NY - 1,),
        grad=(NZ - 1, chunks),
    )
    dma = pltpu.SemaphoreType.DMA
    pairs = {f"{name}_{end}": dma(shape) for name, shape in flights.items() for end in "sr"}
    names = (*inputs, *outputs, *buffers, *pairs, "load")
    return pl.pallas_call(
        functools.partial(layer_kernel, names),
        out_shape=tuple(outputs.values()),
        in_specs=[spec for _, spec in inputs.values()],
        out_specs=[vmem] * len(outputs),
        scratch_shapes=[pltpu.VMEM(*b) for b in buffers.values()] + [*pairs.values(), dma((5,))],
        compiler_params=pltpu.CompilerParams(
            collective_id=0, has_side_effects=True, vmem_limit_bytes=60 << 20
        ),
    )(*(value for value, _ in inputs.values()))


def slot_maps(routes, route_weights, experts):
    tokens = routes.shape[0]
    named = routes[:, :, None] == jnp.arange(experts, dtype=jnp.int32)[None, None, :]
    member = jnp.any(named, axis=1)
    weight = jnp.sum(jnp.where(named, route_weights[:, :, None], 0.0), axis=1)
    earlier = jnp.tril(jnp.ones((tokens, tokens), jnp.bfloat16), -1)
    before = jnp.dot(earlier, member.astype(jnp.bfloat16), preferred_element_type=jnp.float32)
    position = jnp.where(member, before.astype(jnp.int32), -1)
    return position.T, weight.T


def per_device(
    teacher_in,
    routes,
    route_weights,
    expert_gate_up,
    expert_down,
    student_in,
    norm_gain,
    projector,
    second_moment,
):
    tokens_here = teacher_in.shape[0]
    top_count = routes.shape[1]
    experts = lax.axis_size("expert")
    capacity = min(tokens_here, tokens_here * top_count * 9 // (8 * experts))
    position, weight = slot_maps(routes, route_weights, experts)
    code = jnp.where(position >= 0, position, -tokens_here * experts)
    meta = jnp.stack([code.astype(jnp.float32), weight])
    meta = meta.reshape(2, NX, NZ, 2, tokens_here).transpose(2, 0, 1, 3, 4)
    meta = meta.reshape(NZ, 2, OCT, tokens_here)
    gate_up = expert_gate_up.reshape(expert_gate_up.shape[1], -1)
    return layer(
        teacher_in,
        meta,
        gate_up,
        expert_down[0],
        student_in,
        norm_gain,
        projector,
        second_moment,
        capacity,
    )


def solution(mesh):
    placed = (
        P("expert", None),
        P("expert", None),
        P("expert", None),
        P("expert", None, None, "fsdp"),
        P("expert", "fsdp", None),
        P("expert", None),
        P(),
        P(None, "fsdp"),
        P("expert", "fsdp"),
    )
    return jax.shard_map(
        per_device,
        mesh=mesh,
        in_specs=placed,
        out_specs=(P("expert", None), P("expert", "fsdp")),
        check_vma=False,
    )
```

```python
import functools
import types

import jax
import jax.numpy as jnp
from jax import lax
from jax.experimental import pallas as pl
from jax.experimental.pallas import tpu as pltpu
from jax.sharding import PartitionSpec as P

beta_two = 0.95
MESH = pl.DeviceIdType.MESH
NX, NZ, NY = 4, 8, 4
OCT = 2 * NX
WIDTH = 256
ORDER = (0, 1, 2, 6, 4, 5, 3, 7)


def remote(src, dst, send_sem, recv_sem, expert, share):
    return pltpu.make_async_remote_copy(
        src_ref=src,
        dst_ref=dst,
        send_sem=send_sem,
        recv_sem=recv_sem,
        device_id=(expert, share),
        device_id_type=MESH,
    )


class Place:
    def __init__(self):
        expert = lax.axis_index("expert")
        self.y = lax.axis_index("fsdp")
        self.x = expert // (2 * NZ)
        self.z = lax.rem(expert // 2, NZ)
        self.k = lax.rem(expert, 2)

    def at(self, dx=0, dz=0, dk=0):
        x = lax.rem(self.x + dx, NX)
        z = lax.rem(self.z + dz, NZ)
        k = lax.rem(self.k + dk, 2)
        return (x * NZ + z) * 2 + k

    def member(self, dx=0, dk=0):
        return lax.rem(self.x + dx, NX) * 2 + lax.rem(self.k + dk, 2)


def greet(place):
    barrier = pltpu.get_barrier_semaphore()
    peers = [(place.at(dx=dx, dk=dk), place.y) for dx in range(NX) for dk in range(2) if dx or dk]
    peers += [(place.at(dz=dz), place.y) for dz in range(1, NZ)]
    peers += [(place.at(), lax.rem(place.y + dy, NY)) for dy in range(1, NY)]
    for peer in peers:
        pl.semaphore_signal(barrier, inc=1, device_id=peer, device_id_type=MESH)
    return barrier, len(peers)


def cut_of(n, width):
    return slice(n * width, (n + 1) * width)


def part_of(index, size):
    return pl.ds(pl.multiple_of(index * size, size), size)


def norm(wide):
    inv = lax.rsqrt(jnp.mean(wide * wide, axis=1, keepdims=True) + 1e-06)
    return inv, wide * inv


def dot(a, b):
    return jnp.dot(a, b, preferred_element_type=jnp.float32)


class Gather:
    def __init__(self, place, send, landed, ref, tokens, width, sems):
        self.place, self.send, self.landed = place, send, landed
        self.ref, self.tokens, self.width = ref, tokens, width
        self.near_s, self.near_r, self.pass_s, self.pass_r = sems

    def slot(self, c, dx=0, dk=0):
        at = part_of(self.place.member(dx, dk), self.tokens)
        return self.ref.at[at, cut_of(c, self.width)]

    def start(self, c):
        own = self.slot(c)
        for i, dx, dk in ((2, 2, 0), (1, 1, 0), (3, NX - 1, 0), (0, 0, 1)):
            to = self.place.at(dx=dx, dk=dk)
            self.send(own, own, self.near_s.at[i, c], self.near_r.at[i, c], to, self.place.y)

    def onward(self, c):
        for i in (1, 3, 2):
            arrived = self.slot(c, NX - i)
            self.landed(arrived, self.near_s.at[i, c], self.near_r.at[i, c])
            to = self.place.at(dk=1)
            self.send(
                arrived, arrived, self.pass_s.at[i - 1, c], self.pass_r.at[i - 1, c], to, self.place.y
            )

    def finish(self, c):
        self.landed(self.slot(c, 0, 1), self.near_s.at[0, c], self.near_r.at[0, c])
        for i in (1, 3, 2):
            self.landed(self.slot(c, NX - i, 1), self.pass_s.at[i - 1, c], self.pass_r.at[i - 1, c])


def layer_kernel(names, *refs):
    r = types.SimpleNamespace(**dict(zip(names, refs)))
    place = Place()
    y = place.y
    tokens, features = r.student.shape
    part = r.projector.shape[1]
    units = r.down.shape[0]
    block = r.rows.shape[2]
    piece = r.step.shape[0]
    share_rows = tokens // NY
    chunks = part // WIDTH
    f32, bf16 = jnp.float32, jnp.bfloat16
    mine = place.member()
    steps = len(ORDER)
    after, ahead = lax.rem(y + 1, NY), lax.rem(y + NY - 1, NY)

    capacity = block // NZ
    far_share = lax.rem(y + 2, NY)
    loads = [
        pltpu.make_async_copy(
            r.teacher_in.at[:, part_of(y, part)], r.tok.at[0, cut_of(0, tokens)], r.load.at[0]
        ),
        pltpu.make_async_copy(
            r.teacher_in.at[:, part_of(far_share, part)], r.tok.at[1, cut_of(0, tokens)], r.load.at[1]
        ),
        pltpu.make_async_copy(r.projector, r.proj, r.load.at[2]),
        pltpu.make_async_copy(r.gate_up, r.gates, r.load.at[3]),
        pltpu.make_async_copy(r.down.at[:, part_of(y, part)], r.down_all.at[0], r.load.at[4]),
    ]
    barrier, peers = greet(place)
    for load in loads:
        load.start()
    gain = r.gain[...]
    feat = norm(r.student[...].astype(f32))[1] * gain
    r.feat[...] = feat.astype(bf16)
    pl.semaphore_wait(barrier, peers)
    sends = []

    def send(*args):
        copy = remote(*args)
        copy.start()
        sends.append(copy)

    def landed(ref, send_sem, recv_sem):
        remote(ref, ref, send_sem, recv_sem, place.at(), y).wait_recv()

    members = [(dx, dk) for dx in range(NX) for dk in range(2) if dx or dk]

    half = part // 2

    def ring_slot(q, way, hops, c):
        d = hops if way == 0 else (NZ - hops) % NZ
        return r.tok.at[q, cut_of(d, tokens), cut_of(c, half)]

    def ring_send(q, way, hops, c):
        i = way * NZ + hops * 2 + c
        send(
            ring_slot(q, way, hops, c),
            ring_slot(q, way, hops + 1, c),
            r.tok_s.at[q, i],
            r.tok_r.at[q, i],
            place.at(dz=1 if way == 0 else NZ - 1),
            y,
        )

    def ring_start(q):
        for c in range(2):
            for way in range(2):
                ring_send(q, way, 0, c)

    def ring_step(q, hops):
        for c in range(2):
            for way in range(2):
                if hops < NZ // 2 or c == way:
                    i = way * NZ + (hops - 1) * 2 + c
                    landed(ring_slot(q, way, hops, c), r.tok_s.at[q, i], r.tok_r.at[q, i])
                if hops < NZ // 2 - 1 or (hops == NZ // 2 - 1 and c == way):
                    ring_send(q, way, hops, c)

    for dz in range(1, NZ):
        send(
            r.meta.at[lax.rem(place.z + dz, NZ)],
            r.metas.at[dz],
            r.meta_s.at[dz - 1],
            r.meta_r.at[dz - 1],
            place.at(dz=dz),
            y,
        )
    loads[0].wait()
    ring_start(0)
    for dy in (2, 1, 3):
        to = lax.rem(y + dy, NY)
        send(
            r.down.at[:, part_of(to, part)],
            r.down_all.at[dy],
            r.down_s.at[dy - 1],
            r.down_r.at[dy - 1],
            place.at(),
            to,
        )
    r.metas[0] = r.meta[place.z]
    ring_step(0, 1)

    ring_step(0, 2)

    for x in range(NX):
        for z in range(NZ):
            for k in range(2):
                at = ((x * NZ + z) * 2 + k) * piece
                if at % tokens == 0:
                    turned = feat[:, at : at + tokens].T.astype(bf16)
                r.slab[x * 2 + k, z * piece : (z + 1) * piece, :] = turned[
                    at % tokens : at % tokens + piece
                ]
    ring_step(0, 3)
    loads[1].wait()
    ring_start(1)
    for dz in range(1, NZ):
        landed(r.metas.at[dz], r.meta_s.at[dz - 1], r.meta_r.at[dz - 1])
    ring_step(0, 4)

    number = lax.broadcasted_iota(jnp.int32, (block, tokens), 0).astype(f32)

    def expert_at(i):
        return pl.ds(place.member(i // 2, i % 2), 1)

    def select_rows(q, i):
        for d in range(NZ):
            code = r.metas[d, 0, expert_at(i), :] + float(d * capacity)
            r.select[:, cut_of(d, tokens)] = jnp.where(number == code, 1.0, 0.0).astype(bf16)
        picked = dot(r.select[...], r.tok[q]).astype(bf16)
        if i == 0:
            r.rows[2 * q, 0] = picked
        else:
            r.out[q, i - 1] = picked
            send(
                r.out.at[q, i - 1],
                r.rows.at[2 * q, i],
                r.x_s.at[q, i - 1],
                r.x_r.at[q, i - 1],
                place.at(dx=i // 2, dk=i % 2),
                y,
            )

    def pass_rows(j):
        i = ORDER[j]
        if i:
            landed(r.rows.at[0, i], r.x_s.at[0, i - 1], r.x_r.at[0, i - 1])
        send(r.rows.at[0, i], r.rows.at[1, i], r.up_s.at[i], r.up_r.at[i], place.at(), after)
        send(r.rows.at[0, i], r.rows.at[3, i], r.low_s.at[i], r.low_r.at[i], place.at(), ahead)

    for j in range(steps):
        select_rows(0, ORDER[j])
        if j == 0:
            pass_rows(0)
        if j % 2 == 1:
            ring_step(1, (j + 1) // 2)
        if j >= 3:
            pass_rows(j - 2)
    for j in range(steps):
        select_rows(1, ORDER[j])
        if j < 2:
            pass_rows(steps - 2 + j)

    slot = part_of(mine, tokens)
    for i, (dx, dk) in enumerate(members):
        send(
            r.slab.at[place.member(dx, dk)],
            r.slabs.at[:, slot],
            r.slab_s.at[i],
            r.slab_r.at[i],
            place.at(dx=dx, dk=dk),
            y,
        )
    r.slabs[:, slot] = r.slab[mine]
    for load in loads[2:]:
        load.wait()

    def first_product(j):
        i = ORDER[j]
        if i:
            landed(r.rows.at[2, i], r.x_s.at[1, i - 1], r.x_r.at[1, i - 1])
        landed(r.rows.at[1, i], r.up_s.at[i], r.up_r.at[i])
        landed(r.rows.at[3, i], r.low_s.at[i], r.low_r.at[i])
        out = jnp.zeros((block, 2 * units), f32)
        for ry in range(NY):
            share = lax.rem(y + NY - ry, NY)
            out += dot(r.rows[ry, i], r.gates[part_of(share, part), :])
        gate, up = out[:, :units], out[:, units:]
        r.hidden[0, i] = (gate / (1.0 + jnp.exp(-gate)) * up).astype(bf16)
        for dy, to in ((1, after), (3, ahead)):
            send(
                r.hidden.at[0, i], r.hidden.at[dy, i], r.hid_s.at[dy, i], r.hid_r.at[dy, i], place.at(), to
            )

    def relay_hidden(j):
        i = ORDER[j]
        for dy in (1, 3):
            landed(r.hidden.at[dy, i], r.hid_s.at[dy, i], r.hid_r.at[dy, i])
        source, to = (1, after) if j % 2 == 0 else (3, ahead)
        send(r.hidden.at[source, i], r.hidden.at[2, i], r.hid_s.at[2, i], r.hid_r.at[2, i], place.at(), to)

    def second_product(j):
        i = ORDER[j]
        landed(r.hidden.at[2, i], r.hid_s.at[2, i], r.hid_r.at[2, i])
        out = jnp.zeros((block, part), f32)
        for ry in range(NY):
            out += dot(r.hidden[ry, i], r.down_all[ry])
        if i == 0:
            r.home[0:block, :] = out.astype(bf16)
        else:
            r.back[i - 1] = out.astype(bf16)
            send(
                r.back.at[i - 1],
                r.home.at[cut_of(i, block)],
                r.ret_s.at[i - 1],
                r.ret_r.at[i - 1],
                place.at(dx=NX - i // 2, dk=i % 2),
                y,
            )

    def weigh(d):
        pieces = []
        for i in range(OCT):
            code = r.metas[d, 0, expert_at(i), :] + float(d * capacity)
            pieces.append(jnp.where(number == code, r.metas[d, 1, expert_at(i), :], 0.0))
        r.spread[cut_of(d, tokens), :] = jnp.concatenate(pieces, axis=0).T.astype(bf16)

    for j in range(steps + 2):
        if j < steps:
            first_product(j)
        if 0 <= j - 1 < steps:
            relay_hidden(j - 1)
        if j == 1:
            for n in range(chunks):
                r.dense[:, cut_of(n, WIDTH)] = dot(r.feat[...], r.proj[:, cut_of(n, WIDTH)])
        if j == 2:
            for dy in range(1, NY):
                landed(r.down_all.at[dy], r.down_s.at[dy - 1], r.down_r.at[dy - 1])
        if 0 <= j - 2 < steps:
            second_product(j - 2)
        if j < steps:
            weigh(j)

    for i in range(1, OCT):
        landed(r.home.at[cut_of(i, block)], r.ret_s.at[i - 1], r.ret_r.at[i - 1])

    def sum_hop(n, way, left):
        d = left if way == 0 else NZ - left
        here = r.total[n, cut_of(d, tokens), :]
        if left < NZ // 2 - 1 or (left == NZ // 2 - 1 and n % 2 == way):
            i = left * chunks + n
            landed(r.sum_in.at[way, left, n], r.sum_s.at[way, i], r.sum_r.at[way, i])
            here += r.sum_in[way, left, n].astype(f32)
        r.sum_out[way, left - 1, n] = here.astype(bf16)
        i = (left - 1) * chunks + n
        send(
            r.sum_out.at[way, left - 1, n],
            r.sum_in.at[way, left - 1, n],
            r.sum_s.at[way, i],
            r.sum_r.at[way, i],
            place.at(dz=NZ - 1 if way == 0 else 1),
            y,
        )

    res = Gather(
        place, send, landed, r.residue, tokens, WIDTH, (r.res_s, r.res_r, r.resf_s, r.resf_r)
    )
    def sum_rows(n):
        res.finish(n)
        grad = dot(r.slabs[...], r.residue[:, cut_of(n, WIDTH)]).reshape(NZ, piece, WIDTH)
        r.grad[n] = grad.astype(bf16)
        r.own_grad[n] = grad
        for dz in (4, 3, 5, 2, 6, 1, 7):
            send(
                r.grad.at[n, lax.rem(place.z + dz, NZ)],
                r.grads.at[dz - 1, n],
                r.grad_s.at[dz - 1, n],
                r.grad_r.at[dz - 1, n],
                place.at(dz=dz),
                y,
            )

    for i, (dx, dk) in enumerate(members):
        at = part_of(place.member(NX - dx, dk), tokens)
        landed(r.slabs.at[:, at], r.slab_s.at[i], r.slab_r.at[i])
    for wave in range(chunks + NZ // 2 + 2):
        if wave < chunks:
            r.total[wave] = dot(r.spread[...], r.home[:, cut_of(wave, WIDTH)])
        for n in range(chunks):
            hop = wave - n
            left = NZ // 2 - hop
            if hop == 0:
                sum_hop(n, n % 2, left)
            elif 0 < hop < NZ // 2:
                sum_hop(n, 0, left)
                sum_hop(n, 1, left)
            elif hop == NZ // 2:
                teacher = r.total[n, :tokens, :]
                for way in range(2):
                    landed(r.sum_in.at[way, 0, n], r.sum_s.at[way, n], r.sum_r.at[way, n])
                    teacher += r.sum_in[way, 0, n].astype(f32)
                cut = cut_of(n, WIDTH)
                r.residue[slot, cut] = (r.dense[:, cut] - teacher).astype(bf16)
                res.start(n)
            elif hop == NZ // 2 + 1:
                res.onward(n)
            elif hop == NZ // 2 + 2:
                sum_rows(n)
    for n in range(features // WIDTH):
        r.part[:, cut_of(n, WIDTH)] = lax.dot_general(
            r.residue[slot, :],
            r.proj[cut_of(n, WIDTH), :],
            (((1,), (1,)), ((), ())),
            preferred_element_type=f32,
        ).astype(bf16)
    for dy in (2, 1, 3):
        to = lax.rem(y + dy, NY)
        send(
            r.part.at[part_of(to, share_rows)],
            r.parts.at[dy - 1],
            r.part_s.at[dy - 1],
            r.part_r.at[dy - 1],
            place.at(),
            to,
        )

    own_rows = part_of(y, share_rows)
    feat_grad = r.part[own_rows, :].astype(f32)
    for dy in range(1, NY):
        landed(r.parts.at[dy - 1], r.part_s.at[dy - 1], r.part_r.at[dy - 1])
        feat_grad += r.parts[dy - 1].astype(f32)
    inv, normed = norm(r.student[own_rows, :].astype(f32))
    scaled = feat_grad * gain
    r.d_own[...] = (
        inv * (scaled - normed * jnp.mean(scaled * normed, axis=1, keepdims=True))
    ).astype(bf16)
    for dy in (2, 1, 3):
        to = lax.rem(y + dy, NY)
        send(r.d_own, r.d_all.at[dy - 1], r.d_s.at[dy - 1], r.d_r.at[dy - 1], place.at(), to)
    r.d[own_rows, :] = r.d_own[...]

    for n in range(chunks):
        total = r.own_grad[n, place.z]
        for dz in (1, 7, 2, 6, 3, 5, 4):
            landed(r.grads.at[dz - 1, n], r.grad_s.at[dz - 1, n], r.grad_r.at[dz - 1, n])
            total += r.grads[dz - 1, n].astype(f32)
        cut = cut_of(n, WIDTH)
        r.step[:, cut] = total * lax.rsqrt(
            beta_two * r.moment[:, cut] + (1.0 - beta_two) * total * total
        )
    for dy in range(1, NY):
        landed(r.d_all.at[dy - 1], r.d_s.at[dy - 1], r.d_r.at[dy - 1])
        r.d[part_of(lax.rem(y + NY - dy, NY), share_rows), :] = r.d_all[dy - 1]
    for copy in sends:
        copy.wait_send()


def layer(teacher_in, meta, gate_up, down, student_in, norm_gain, projector, second_moment, capacity):
    tokens, features = student_in.shape
    part = projector.shape[1]
    units = down.shape[0]
    block = OCT * capacity
    piece = second_moment.shape[0]
    share_rows = tokens // NY
    chunks = part // WIDTH
    bf16, f32 = jnp.bfloat16, jnp.float32
    vmem, anywhere = pl.BlockSpec(memory_space=pltpu.VMEM), pl.BlockSpec(memory_space=pl.ANY)
    inputs = dict(
        teacher_in=(teacher_in, anywhere),
        meta=(meta, vmem),
        gate_up=(gate_up, anywhere),
        down=(down, anywhere),
        student=(student_in, vmem),
        gain=(norm_gain.reshape(1, -1), vmem),
        projector=(projector, anywhere),
        moment=(second_moment, vmem),
    )
    outputs = dict(
        d=jax.ShapeDtypeStruct((tokens, features), bf16),
        step=jax.ShapeDtypeStruct(second_moment.shape, f32),
    )
    buffers = dict(
        proj=(projector.shape, bf16),
        gates=(gate_up.shape, bf16),
        tok=((2, NZ * tokens, part), bf16),
        metas=(meta.shape, f32),
        select=((block, OCT * tokens), bf16),
        spread=((OCT * tokens, NZ * block), bf16),
        out=((2, OCT - 1, block, part), bf16),
        rows=((NY, NZ, block, part), bf16),
        hidden=((NY, NZ, block, units), bf16),
        down_all=((NY, units, part), bf16),
        back=((NZ - 1, block, part), bf16),
        home=((NZ * block, part), bf16),
        total=((chunks, NZ * tokens, WIDTH), f32),
        sum_out=((2, NZ // 2, chunks, tokens, WIDTH), bf16),
        sum_in=((2, NZ // 2, chunks, tokens, WIDTH), bf16),
        feat=((tokens, features), bf16),
        dense=((tokens, part), f32),
        slab=((OCT, NZ * piece, tokens), bf16),
        slabs=((NZ * piece, OCT * tokens), bf16),
        residue=((OCT * tokens, part), bf16),
        part=((tokens, features), bf16),
        parts=((NY - 1, share_rows, features), bf16),
        d_own=((share_rows, features), bf16),
        d_all=((NY - 1, share_rows, features), bf16),
        grad=((chunks, NZ, piece, WIDTH), bf16),
        grads=((NZ - 1, chunks, piece, WIDTH), bf16),
        own_grad=((chunks, NZ, piece, WIDTH), f32),
    )
    flights = dict(
        meta=(NZ - 1,),
        tok=(2, 2 * NZ),
        down=(NY - 1,),
        x=(2, OCT - 1),
        up=(OCT,),
        low=(OCT,),
        hid=(NY, OCT),
        ret=(OCT - 1,),
        sum=(2, NZ // 2 * chunks),
        slab=(OCT - 1,),
        res=(4, chunks),
        resf=(3, chunks),
        part=(NY - 1,),
        d=(NY - 1,),
        grad=(NZ - 1, chunks),
    )
    dma = pltpu.SemaphoreType.DMA
    pairs = {f"{name}_{end}": dma(shape) for name, shape in flights.items() for end in "sr"}
    names = (*inputs, *outputs, *buffers, *pairs, "load")
    return pl.pallas_call(
        functools.partial(layer_kernel, names),
        out_shape=tuple(outputs.values()),
        in_specs=[spec for _, spec in inputs.values()],
        out_specs=[vmem] * len(outputs),
        scratch_shapes=[pltpu.VMEM(*b) for b in buffers.values()] + [*pairs.values(), dma((5,))],
        compiler_params=pltpu.CompilerParams(
            collective_id=0, has_side_effects=True, vmem_limit_bytes=60 << 20
        ),
    )(*(value for value, _ in inputs.values()))


def slot_maps(routes, route_weights, experts):
    tokens = routes.shape[0]
    named = routes[:, :, None] == jnp.arange(experts, dtype=jnp.int32)[None, None, :]
    member = jnp.any(named, axis=1)
    weight = jnp.sum(jnp.where(named, route_weights[:, :, None], 0.0), axis=1)
    earlier = jnp.tril(jnp.ones((tokens, tokens), jnp.bfloat16), -1)
    before = jnp.dot(earlier, member.astype(jnp.bfloat16), preferred_element_type=jnp.float32)
    position = jnp.where(member, before.astype(jnp.int32), -1)
    return position.T, weight.T


def per_device(
    teacher_in,
    routes,
    route_weights,
    expert_gate_up,
    expert_down,
    student_in,
    norm_gain,
    projector,
    second_moment,
):
    tokens_here = teacher_in.shape[0]
    top_count = routes.shape[1]
    experts = lax.axis_size("expert")
    capacity = min(tokens_here, tokens_here * top_count * 9 // (8 * experts))
    position, weight = slot_maps(routes, route_weights, experts)
    code = jnp.where(position >= 0, position, -tokens_here * experts)
    meta = jnp.stack([code.astype(jnp.float32), weight])
    meta = meta.reshape(2, NX, NZ, 2, tokens_here).transpose(2, 0, 1, 3, 4)
    meta = meta.reshape(NZ, 2, OCT, tokens_here)
    gate_up = expert_gate_up.reshape(expert_gate_up.shape[1], -1)
    return layer(
        teacher_in,
        meta,
        gate_up,
        expert_down[0],
        student_in,
        norm_gain,
        projector,
        second_moment,
        capacity,
    )


def solution(mesh):
    placed = (
        P("expert", None),
        P("expert", None),
        P("expert", None),
        P("expert", None, None, "fsdp"),
        P("expert", "fsdp", None),
        P("expert", None),
        P(),
        P(None, "fsdp"),
        P("expert", "fsdp"),
    )
    return jax.shard_map(
        per_device,
        mesh=mesh,
        in_specs=placed,
        out_specs=(P("expert", None), P("expert", "fsdp")),
        check_vma=False,
    )
```

```python
import functools
import types

import jax
import jax.numpy as jnp
from jax import lax
from jax.experimental import pallas as pl
from jax.experimental.pallas import tpu as pltpu
from jax.sharding import PartitionSpec as P

beta_two = 0.95
MESH = pl.DeviceIdType.MESH
NX, NZ, NY = 4, 8, 4
OCT = 2 * NX
WIDTH = 256
UNITS = (0, 1, 3, 2, 4, 6, 5, 7)
DISTANCES = (2, 3, 4, 5, 6, 7, 0, 1)


def remote(src, dst, send_sem, recv_sem, expert, share):
    return pltpu.make_async_remote_copy(
        src_ref=src,
        dst_ref=dst,
        send_sem=send_sem,
        recv_sem=recv_sem,
        device_id=(expert, share),
        device_id_type=MESH,
    )


class Place:
    def __init__(self):
        expert = lax.axis_index("expert")
        self.y = lax.axis_index("fsdp")
        self.x = expert // (2 * NZ)
        self.z = lax.rem(expert // 2, NZ)
        self.k = lax.rem(expert, 2)

    def at(self, dx=0, dz=0, dk=0):
        x = lax.rem(self.x + dx, NX)
        z = lax.rem(self.z + dz, NZ)
        k = lax.rem(self.k + dk, 2)
        return (x * NZ + z) * 2 + k

    def member(self, dx=0, dk=0):
        return lax.rem(self.x + dx, NX) * 2 + lax.rem(self.k + dk, 2)


def greet(place):
    barrier = pltpu.get_barrier_semaphore()
    peers = [(place.at(dx=dx, dk=dk), place.y) for dx in range(NX) for dk in range(2) if dx or dk]
    peers += [(place.at(dz=dz), place.y) for dz in range(1, NZ)]
    peers += [(place.at(), lax.rem(place.y + dy, NY)) for dy in range(1, NY)]
    for peer in peers:
        pl.semaphore_signal(barrier, inc=1, device_id=peer, device_id_type=MESH)
    return barrier, len(peers)


def cut_of(n, width):
    return slice(n * width, (n + 1) * width)


def part_of(index, size):
    return pl.ds(pl.multiple_of(index * size, size), size)


def norm(wide):
    inv = lax.rsqrt(jnp.mean(wide * wide, axis=1, keepdims=True) + 1e-06)
    return inv, wide * inv


def dot(a, b):
    return jnp.dot(a, b, preferred_element_type=jnp.float32)


class Gather:
    def __init__(self, place, send, landed, ref, tokens, width, sems):
        self.place, self.send, self.landed = place, send, landed
        self.ref, self.tokens, self.width = ref, tokens, width
        self.near_s, self.near_r, self.pass_s, self.pass_r = sems

    def slot(self, c, dx=0, dk=0):
        at = part_of(self.place.member(dx, dk), self.tokens)
        return self.ref.at[at, cut_of(c, self.width)]

    def start(self, c):
        own = self.slot(c)
        for i, dx, dk in ((2, 2, 0), (1, 1, 0), (3, NX - 1, 0), (0, 0, 1)):
            to = self.place.at(dx=dx, dk=dk)
            self.send(own, own, self.near_s.at[i, c], self.near_r.at[i, c], to, self.place.y)

    def onward(self, c):
        for i in (1, 3, 2):
            arrived = self.slot(c, NX - i)
            self.landed(arrived, self.near_s.at[i, c], self.near_r.at[i, c])
            to = self.place.at(dk=1)
            self.send(
                arrived, arrived, self.pass_s.at[i - 1, c], self.pass_r.at[i - 1, c], to, self.place.y
            )

    def finish(self, c):
        self.landed(self.slot(c, 0, 1), self.near_s.at[0, c], self.near_r.at[0, c])
        for i in (1, 3, 2):
            self.landed(self.slot(c, NX - i, 1), self.pass_s.at[i - 1, c], self.pass_r.at[i - 1, c])


def layer_kernel(names, *refs):
    r = types.SimpleNamespace(**dict(zip(names, refs)))
    place = Place()
    y = place.y
    tokens, features = r.student.shape
    part = r.projector.shape[1]
    units = r.down.shape[0]
    block = 2 * r.rows.shape[3]
    piece = r.step.shape[0]
    share_rows = tokens // NY
    chunks = part // WIDTH
    f32, bf16 = jnp.float32, jnp.bfloat16
    mine = place.member()
    steps = len(UNITS)
    after, ahead = lax.rem(y + 1, NY), lax.rem(y + NY - 1, NY)

    capacity = block // NZ
    fours = NZ // 2
    rows = block // 2
    far_share = lax.rem(y + 2, NY)
    loads = [
        pltpu.make_async_copy(
            r.teacher_in.at[:, part_of(y, part)], r.tok.at[0, cut_of(DISTANCES.index(0), tokens)], r.load.at[0]
        ),
        pltpu.make_async_copy(
            r.teacher_in.at[:, part_of(far_share, part)], r.tok.at[1, cut_of(DISTANCES.index(0), tokens)], r.load.at[1]
        ),
        pltpu.make_async_copy(r.projector, r.proj, r.load.at[2]),
        pltpu.make_async_copy(r.gate_up, r.gates, r.load.at[3]),
        pltpu.make_async_copy(r.down.at[:, part_of(y, part)], r.down_all.at[0], r.load.at[4]),
    ]
    barrier, peers = greet(place)
    for load in loads:
        load.start()
    gain = r.gain[...]
    feat = norm(r.student[...].astype(f32))[1] * gain
    r.feat[...] = feat.astype(bf16)
    pl.semaphore_wait(barrier, peers)
    sends = []

    def send(*args):
        copy = remote(*args)
        copy.start()
        sends.append(copy)

    def landed(ref, send_sem, recv_sem):
        remote(ref, ref, send_sem, recv_sem, place.at(), y).wait_recv()

    members = [(dx, dk) for dx in range(NX) for dk in range(2) if dx or dk]

    half = part // 2

    def ring_slot(q, way, hops, c):
        d = hops if way == 0 else (NZ - hops) % NZ
        return r.tok.at[q, cut_of(DISTANCES.index(d), tokens), cut_of(c, half)]

    def ring_send(q, way, hops, c):
        i = way * NZ + hops * 2 + c
        send(
            ring_slot(q, way, hops, c),
            ring_slot(q, way, hops + 1, c),
            r.tok_s.at[q, i],
            r.tok_r.at[q, i],
            place.at(dz=1 if way == 0 else NZ - 1),
            y,
        )

    def ring_start(q):
        for c in range(2):
            for way in range(2):
                ring_send(q, way, 0, c)

    def ring_step(q, hops):
        for c in range(2):
            for way in range(2):
                if hops < NZ // 2 or c == way:
                    i = way * NZ + (hops - 1) * 2 + c
                    landed(ring_slot(q, way, hops, c), r.tok_s.at[q, i], r.tok_r.at[q, i])
                if hops < NZ // 2 - 1 or (hops == NZ // 2 - 1 and c == way):
                    ring_send(q, way, hops, c)

    for dz in range(1, NZ):
        send(
            r.meta.at[lax.rem(place.z + dz, NZ)],
            r.metas.at[dz],
            r.meta_s.at[dz - 1],
            r.meta_r.at[dz - 1],
            place.at(dz=dz),
            y,
        )
    loads[0].wait()
    ring_start(0)
    for dy in (2, 1, 3):
        to = lax.rem(y + dy, NY)
        send(
            r.down.at[:, part_of(to, part)],
            r.down_all.at[dy],
            r.down_s.at[dy - 1],
            r.down_r.at[dy - 1],
            place.at(),
            to,
        )
    r.metas[0] = r.meta[place.z]
    ring_step(0, 1)

    ring_step(0, 2)

    for x in range(NX):
        for z in range(NZ):
            for k in range(2):
                at = ((x * NZ + z) * 2 + k) * piece
                if at % tokens == 0:
                    turned = feat[:, at : at + tokens].T.astype(bf16)
                r.slab[x * 2 + k, z * piece : (z + 1) * piece, :] = turned[
                    at % tokens : at % tokens + piece
                ]
    ring_step(0, 3)
    loads[1].wait()
    ring_start(1)
    for dz in range(1, NZ):
        landed(r.metas.at[dz], r.meta_s.at[dz - 1], r.meta_r.at[dz - 1])
    ring_step(0, 4)

    number = lax.broadcasted_iota(jnp.int32, (rows, tokens), 0).astype(f32)

    def expert_at(i):
        return pl.ds(place.member(i // 2, i % 2), 1)

    def select_rows(q, u):
        group, dx = u // NX, u % NX
        for i in range(fours):
            d = DISTANCES[group * fours + i]
            pieces = []
            for dk in range(2):
                code = r.metas[d, 0, expert_at(2 * dx + dk), :] + float(i * capacity)
                pieces.append(jnp.where(number == code, 1.0, 0.0))
            r.select[:, cut_of(i, tokens)] = jnp.concatenate(pieces, axis=0).astype(bf16)
        picked = dot(r.select[...], r.tok[q, cut_of(group, fours * tokens)])
        for dk in range(2):
            if dx or dk:
                r.out[q, u, dk] = picked[cut_of(dk, rows)].astype(bf16)
                send(
                    r.out.at[q, u, dk],
                    r.rows.at[2 * q, u, dk],
                    r.x_s.at[q, 2 * u + dk],
                    r.x_r.at[q, 2 * u + dk],
                    place.at(dx=dx, dk=dk),
                    y,
                )
            else:
                r.rows[2 * q, u, dk] = picked[cut_of(dk, rows)].astype(bf16)

    def rows_landed(q, u):
        for dk in range(2):
            if u % NX or dk:
                at = r.rows.at[2 * q, u, dk]
                landed(at, r.x_s.at[q, 2 * u + dk], r.x_r.at[q, 2 * u + dk])

    def pass_rows(j):
        u = UNITS[j]
        rows_landed(0, u)
        send(r.rows.at[0, u], r.rows.at[1, u], r.up_s.at[u], r.up_r.at[u], place.at(), after)
        send(r.rows.at[0, u], r.rows.at[3, u], r.low_s.at[u], r.low_r.at[u], place.at(), ahead)

    for j in range(steps):
        select_rows(0, UNITS[j])
        if j % 2 == 1:
            ring_step(1, (j + 1) // 2)
        if j >= 1:
            pass_rows(j - 1)
    for j in range(steps):
        select_rows(1, UNITS[j])
        if j == 0:
            pass_rows(steps - 1)

    slot = part_of(mine, tokens)
    for i, (dx, dk) in enumerate(members):
        send(
            r.slab.at[place.member(dx, dk)],
            r.slabs.at[:, slot],
            r.slab_s.at[i],
            r.slab_r.at[i],
            place.at(dx=dx, dk=dk),
            y,
        )
    r.slabs[:, slot] = r.slab[mine]
    for load in loads[2:]:
        load.wait()

    def first_product(j):
        i = UNITS[j]
        rows_landed(1, i)
        landed(r.rows.at[1, i], r.up_s.at[i], r.up_r.at[i])
        landed(r.rows.at[3, i], r.low_s.at[i], r.low_r.at[i])
        out = jnp.zeros((block, 2 * units), f32)
        for ry in range(NY):
            share = lax.rem(y + NY - ry, NY)
            out += dot(r.rows[ry, i].reshape(block, part), r.gates[part_of(share, part), :])
        gate, up = out[:, :units], out[:, units:]
        r.hidden[0, i] = (gate / (1.0 + jnp.exp(-gate)) * up).astype(bf16)
        for dy, to in ((1, after), (3, ahead)):
            send(
                r.hidden.at[0, i], r.hidden.at[dy, i], r.hid_s.at[dy, i], r.hid_r.at[dy, i], place.at(), to
            )

    def relay_hidden(j):
        i = UNITS[j]
        for dy in (1, 3):
            landed(r.hidden.at[dy, i], r.hid_s.at[dy, i], r.hid_r.at[dy, i])
        source, to = (1, after) if j % 2 == 0 else (3, ahead)
        send(r.hidden.at[source, i], r.hidden.at[2, i], r.hid_s.at[2, i], r.hid_r.at[2, i], place.at(), to)

    def second_product(j):
        u = UNITS[j]
        dx = u % NX
        landed(r.hidden.at[2, u], r.hid_s.at[2, u], r.hid_r.at[2, u])
        out = jnp.zeros((block, part), f32)
        for ry in range(NY):
            out += dot(r.hidden[ry, u], r.down_all[ry])
        for dk in range(2):
            if dx or dk:
                r.back[u, dk] = out[cut_of(dk, rows)].astype(bf16)
                send(
                    r.back.at[u, dk],
                    r.home.at[2 * u + dk],
                    r.ret_s.at[2 * u + dk],
                    r.ret_r.at[2 * u + dk],
                    place.at(dx=NX - dx, dk=dk),
                    y,
                )
            else:
                r.home[2 * u + dk] = out[cut_of(dk, rows)].astype(bf16)

    def weigh(j):
        group, i = j // fours, j % fours
        d = DISTANCES[j]
        pieces = []
        for o in range(OCT):
            code = r.metas[d, 0, expert_at(o), :] + float(i * capacity)
            pieces.append(jnp.where(number == code, r.metas[d, 1, expert_at(o), :], 0.0))
        r.spread[group, cut_of(i, tokens), :] = jnp.concatenate(pieces, axis=0).T.astype(bf16)

    def came_home(group):
        for u in range(group * NX, (group + 1) * NX):
            for dk in range(2):
                if u % NX or dk:
                    landed(r.home.at[2 * u + dk], r.ret_s.at[2 * u + dk], r.ret_r.at[2 * u + dk])

    def combine(group, n):
        r.total[n, cut_of(group, fours * tokens), :] = dot(
            r.spread[group], r.home[cut_of(group, OCT), :, cut_of(n, WIDTH)].reshape(NX * block, WIDTH)
        )

    def sum_hop(n, way, left):
        d = left if way == 0 else NZ - left
        here = r.total[n, cut_of(DISTANCES.index(d), tokens), :]
        if left < NZ // 2 - 1 or (left == NZ // 2 - 1 and n % 2 == way):
            i = left * chunks + n
            landed(r.sum_in.at[way, left, n], r.sum_s.at[way, i], r.sum_r.at[way, i])
            here += r.sum_in[way, left, n].astype(f32)
        r.sum_out[way, left - 1, n] = here.astype(bf16)
        i = (left - 1) * chunks + n
        send(
            r.sum_out.at[way, left - 1, n],
            r.sum_in.at[way, left - 1, n],
            r.sum_s.at[way, i],
            r.sum_r.at[way, i],
            place.at(dz=NZ - 1 if way == 0 else 1),
            y,
        )

    for j in range(steps + 2):
        if j < steps:
            first_product(j)
        if 0 <= j - 1 < steps:
            relay_hidden(j - 1)
        if j == 1:
            for n in range(chunks):
                r.dense[:, cut_of(n, WIDTH)] = dot(r.feat[...], r.proj[:, cut_of(n, WIDTH)])
        if j == 2:
            for dy in range(1, NY):
                landed(r.down_all.at[dy], r.down_s.at[dy - 1], r.down_r.at[dy - 1])
        if 0 <= j - 2 < steps:
            second_product(j - 2)
        if j < steps:
            weigh(j)
        if j == NX + 2:
            came_home(0)
            for n in range(chunks):
                combine(0, n)
                sum_hop(n, n % 2, 4)
        if j == NX + 3:
            for n in range(chunks):
                sum_hop(n, 0, 3)
                sum_hop(n, 1, 3)
        if j == NX + 4:
            for n in range(chunks):
                sum_hop(n, 0, 2)
    came_home(1)

    res = Gather(
        place, send, landed, r.residue, tokens, WIDTH, (r.res_s, r.res_r, r.resf_s, r.resf_r)
    )
    def sum_rows(n):
        res.finish(n)
        grad = dot(r.slabs[...], r.residue[:, cut_of(n, WIDTH)]).reshape(NZ, piece, WIDTH)
        r.grad[n] = grad.astype(bf16)
        r.own_grad[n] = grad
        for dz in (4, 3, 5, 2, 6, 1, 7):
            send(
                r.grad.at[n, lax.rem(place.z + dz, NZ)],
                r.grads.at[dz - 1, n],
                r.grad_s.at[dz - 1, n],
                r.grad_r.at[dz - 1, n],
                place.at(dz=dz),
                y,
            )

    for i, (dx, dk) in enumerate(members):
        at = part_of(place.member(NX - dx, dk), tokens)
        landed(r.slabs.at[:, at], r.slab_s.at[i], r.slab_r.at[i])
    for wave in range(chunks + 4):
        for n in reversed(range(chunks)):
            stage = wave - n
            if stage == 0:
                combine(1, n)
                sum_hop(n, 1, 2)
            elif stage == 1:
                sum_hop(n, 0, 1)
                sum_hop(n, 1, 1)
            elif stage == 2:
                teacher = r.total[n, cut_of(DISTANCES.index(0), tokens), :]
                for way in range(2):
                    landed(r.sum_in.at[way, 0, n], r.sum_s.at[way, n], r.sum_r.at[way, n])
                    teacher += r.sum_in[way, 0, n].astype(f32)
                cut = cut_of(n, WIDTH)
                r.residue[slot, cut] = (r.dense[:, cut] - teacher).astype(bf16)
                res.start(n)
            elif stage == 3:
                res.onward(n)
            elif stage == 4:
                sum_rows(n)
        if wave == chunks + 1:
            for n in range(features // WIDTH):
                r.part[:, cut_of(n, WIDTH)] = lax.dot_general(
                    r.residue[slot, :],
                    r.proj[cut_of(n, WIDTH), :],
                    (((1,), (1,)), ((), ())),
                    preferred_element_type=f32,
                ).astype(bf16)
            for dy in (2, 1, 3):
                to = lax.rem(y + dy, NY)
                send(
                    r.part.at[part_of(to, share_rows)],
                    r.parts.at[dy - 1],
                    r.part_s.at[dy - 1],
                    r.part_r.at[dy - 1],
                    place.at(),
                    to,
                )


    own_rows = part_of(y, share_rows)
    feat_grad = r.part[own_rows, :].astype(f32)
    for dy in range(1, NY):
        landed(r.parts.at[dy - 1], r.part_s.at[dy - 1], r.part_r.at[dy - 1])
        feat_grad += r.parts[dy - 1].astype(f32)
    inv, normed = norm(r.student[own_rows, :].astype(f32))
    scaled = feat_grad * gain
    r.d_own[...] = (
        inv * (scaled - normed * jnp.mean(scaled * normed, axis=1, keepdims=True))
    ).astype(bf16)
    for dy in (2, 1, 3):
        to = lax.rem(y + dy, NY)
        send(r.d_own, r.d_all.at[dy - 1], r.d_s.at[dy - 1], r.d_r.at[dy - 1], place.at(), to)
    r.d[own_rows, :] = r.d_own[...]

    for n in range(chunks):
        total = r.own_grad[n, place.z]
        for dz in (1, 7, 2, 6, 3, 5, 4):
            landed(r.grads.at[dz - 1, n], r.grad_s.at[dz - 1, n], r.grad_r.at[dz - 1, n])
            total += r.grads[dz - 1, n].astype(f32)
        cut = cut_of(n, WIDTH)
        r.step[:, cut] = total * lax.rsqrt(
            beta_two * r.moment[:, cut] + (1.0 - beta_two) * total * total
        )
    for dy in range(1, NY):
        landed(r.d_all.at[dy - 1], r.d_s.at[dy - 1], r.d_r.at[dy - 1])
        r.d[part_of(lax.rem(y + NY - dy, NY), share_rows), :] = r.d_all[dy - 1]
    for copy in sends:
        copy.wait_send()


def layer(teacher_in, meta, gate_up, down, student_in, norm_gain, projector, second_moment, capacity):
    tokens, features = student_in.shape
    part = projector.shape[1]
    units = down.shape[0]
    block = OCT * capacity
    piece = second_moment.shape[0]
    share_rows = tokens // NY
    chunks = part // WIDTH
    bf16, f32 = jnp.bfloat16, jnp.float32
    vmem, anywhere = pl.BlockSpec(memory_space=pltpu.VMEM), pl.BlockSpec(memory_space=pl.ANY)
    inputs = dict(
        teacher_in=(teacher_in, anywhere),
        meta=(meta, vmem),
        gate_up=(gate_up, anywhere),
        down=(down, anywhere),
        student=(student_in, vmem),
        gain=(norm_gain.reshape(1, -1), vmem),
        projector=(projector, anywhere),
        moment=(second_moment, vmem),
    )
    outputs = dict(
        d=jax.ShapeDtypeStruct((tokens, features), bf16),
        step=jax.ShapeDtypeStruct(second_moment.shape, f32),
    )
    buffers = dict(
        proj=(projector.shape, bf16),
        gates=(gate_up.shape, bf16),
        tok=((2, NZ * tokens, part), bf16),
        metas=(meta.shape, f32),
        select=((block, NZ // 2 * tokens), bf16),
        spread=((2, NZ // 2 * tokens, NX * block), bf16),
        out=((2, OCT, 2, block // 2, part), bf16),
        rows=((NY, OCT, 2, block // 2, part), bf16),
        hidden=((NY, NZ, block, units), bf16),
        down_all=((NY, units, part), bf16),
        back=((OCT, 2, block // 2, part), bf16),
        home=((2 * OCT, block // 2, part), bf16),
        total=((chunks, NZ * tokens, WIDTH), f32),
        sum_out=((2, NZ // 2, chunks, tokens, WIDTH), bf16),
        sum_in=((2, NZ // 2, chunks, tokens, WIDTH), bf16),
        feat=((tokens, features), bf16),
        dense=((tokens, part), f32),
        slab=((OCT, NZ * piece, tokens), bf16),
        slabs=((NZ * piece, OCT * tokens), bf16),
        residue=((OCT * tokens, part), bf16),
        part=((tokens, features), bf16),
        parts=((NY - 1, share_rows, features), bf16),
        d_own=((share_rows, features), bf16),
        d_all=((NY - 1, share_rows, features), bf16),
        grad=((chunks, NZ, piece, WIDTH), bf16),
        grads=((NZ - 1, chunks, piece, WIDTH), bf16),
        own_grad=((chunks, NZ, piece, WIDTH), f32),
    )
    flights = dict(
        meta=(NZ - 1,),
        tok=(2, 2 * NZ),
        down=(NY - 1,),
        x=(2, 2 * OCT),
        up=(OCT,),
        low=(OCT,),
        hid=(NY, OCT),
        ret=(2 * OCT,),
        sum=(2, NZ // 2 * chunks),
        slab=(OCT - 1,),
        res=(4, chunks),
        resf=(3, chunks),
        part=(NY - 1,),
        d=(NY - 1,),
        grad=(NZ - 1, chunks),
    )
    dma = pltpu.SemaphoreType.DMA
    pairs = {f"{name}_{end}": dma(shape) for name, shape in flights.items() for end in "sr"}
    names = (*inputs, *outputs, *buffers, *pairs, "load")
    return pl.pallas_call(
        functools.partial(layer_kernel, names),
        out_shape=tuple(outputs.values()),
        in_specs=[spec for _, spec in inputs.values()],
        out_specs=[vmem] * len(outputs),
        scratch_shapes=[pltpu.VMEM(*b) for b in buffers.values()] + [*pairs.values(), dma((5,))],
        compiler_params=pltpu.CompilerParams(
            collective_id=0, has_side_effects=True, vmem_limit_bytes=60 << 20
        ),
    )(*(value for value, _ in inputs.values()))


def slot_maps(routes, route_weights, experts):
    tokens = routes.shape[0]
    named = routes[:, :, None] == jnp.arange(experts, dtype=jnp.int32)[None, None, :]
    member = jnp.any(named, axis=1)
    weight = jnp.sum(jnp.where(named, route_weights[:, :, None], 0.0), axis=1)
    earlier = jnp.tril(jnp.ones((tokens, tokens), jnp.bfloat16), -1)
    before = jnp.dot(earlier, member.astype(jnp.bfloat16), preferred_element_type=jnp.float32)
    position = jnp.where(member, before.astype(jnp.int32), -1)
    return position.T, weight.T


def per_device(
    teacher_in,
    routes,
    route_weights,
    expert_gate_up,
    expert_down,
    student_in,
    norm_gain,
    projector,
    second_moment,
):
    tokens_here = teacher_in.shape[0]
    top_count = routes.shape[1]
    experts = lax.axis_size("expert")
    capacity = min(tokens_here, tokens_here * top_count * 9 // (8 * experts))
    position, weight = slot_maps(routes, route_weights, experts)
    code = jnp.where(position >= 0, position, -tokens_here * experts)
    meta = jnp.stack([code.astype(jnp.float32), weight])
    meta = meta.reshape(2, NX, NZ, 2, tokens_here).transpose(2, 0, 1, 3, 4)
    meta = meta.reshape(NZ, 2, OCT, tokens_here)
    gate_up = expert_gate_up.reshape(expert_gate_up.shape[1], -1)
    return layer(
        teacher_in,
        meta,
        gate_up,
        expert_down[0],
        student_in,
        norm_gain,
        projector,
        second_moment,
        capacity,
    )


def solution(mesh):
    placed = (
        P("expert", None),
        P("expert", None),
        P("expert", None),
        P("expert", None, None, "fsdp"),
        P("expert", "fsdp", None),
        P("expert", None),
        P(),
        P(None, "fsdp"),
        P("expert", "fsdp"),
    )
    return jax.shard_map(
        per_device,
        mesh=mesh,
        in_specs=placed,
        out_specs=(P("expert", None), P("expert", "fsdp")),
        check_vma=False,
    )
```

```python
import functools
import types

import jax
import jax.numpy as jnp
from jax import lax
from jax.experimental import pallas as pl
from jax.experimental.pallas import tpu as pltpu
from jax.sharding import PartitionSpec as P

beta_two = 0.95
MESH = pl.DeviceIdType.MESH
NX, NZ, NY = 4, 8, 4
OCT = 2 * NX
WIDTH = 256
UNITS = (0, 1, 3, 2, 4, 6, 5, 7)
DISTANCES = (2, 3, 4, 5, 6, 7, 0, 1)


def remote(src, dst, send_sem, recv_sem, expert, share):
    return pltpu.make_async_remote_copy(
        src_ref=src,
        dst_ref=dst,
        send_sem=send_sem,
        recv_sem=recv_sem,
        device_id=(expert, share),
        device_id_type=MESH,
    )


class Place:
    def __init__(self):
        expert = lax.axis_index("expert")
        self.y = lax.axis_index("fsdp")
        self.x = expert // (2 * NZ)
        self.z = lax.rem(expert // 2, NZ)
        self.k = lax.rem(expert, 2)

    def at(self, dx=0, dz=0, dk=0):
        x = lax.rem(self.x + dx, NX)
        z = lax.rem(self.z + dz, NZ)
        k = lax.rem(self.k + dk, 2)
        return (x * NZ + z) * 2 + k

    def member(self, dx=0, dk=0):
        return lax.rem(self.x + dx, NX) * 2 + lax.rem(self.k + dk, 2)


def greet(place):
    barrier = pltpu.get_barrier_semaphore()
    peers = [(place.at(dx=dx, dk=dk), place.y) for dx in range(NX) for dk in range(2) if dx or dk]
    peers += [(place.at(dz=dz), place.y) for dz in range(1, NZ)]
    peers += [(place.at(), lax.rem(place.y + dy, NY)) for dy in range(1, NY)]
    for peer in peers:
        pl.semaphore_signal(barrier, inc=1, device_id=peer, device_id_type=MESH)
    return barrier, len(peers)


def cut_of(n, width):
    return slice(n * width, (n + 1) * width)


def part_of(index, size):
    return pl.ds(pl.multiple_of(index * size, size), size)


def norm(wide):
    inv = lax.rsqrt(jnp.mean(wide * wide, axis=1, keepdims=True) + 1e-06)
    return inv, wide * inv


def dot(a, b):
    return jnp.dot(a, b, preferred_element_type=jnp.float32)


class Gather:
    def __init__(self, place, send, landed, ref, tokens, width, sems):
        self.place, self.send, self.landed = place, send, landed
        self.ref, self.tokens, self.width = ref, tokens, width
        self.near_s, self.near_r, self.pass_s, self.pass_r = sems

    def slot(self, c, dx=0, dk=0):
        at = part_of(self.place.member(dx, dk), self.tokens)
        return self.ref.at[at, cut_of(c, self.width)]

    def start(self, c):
        own = self.slot(c)
        for i, dx, dk in ((2, 2, 0), (1, 1, 0), (3, NX - 1, 0), (0, 0, 1)):
            to = self.place.at(dx=dx, dk=dk)
            self.send(own, own, self.near_s.at[i, c], self.near_r.at[i, c], to, self.place.y)

    def onward(self, c):
        for i in (1, 3, 2):
            arrived = self.slot(c, NX - i)
            self.landed(arrived, self.near_s.at[i, c], self.near_r.at[i, c])
            to = self.place.at(dk=1)
            self.send(
                arrived, arrived, self.pass_s.at[i - 1, c], self.pass_r.at[i - 1, c], to, self.place.y
            )

    def finish(self, c):
        self.landed(self.slot(c, 0, 1), self.near_s.at[0, c], self.near_r.at[0, c])
        for i in (1, 3, 2):
            self.landed(self.slot(c, NX - i, 1), self.pass_s.at[i - 1, c], self.pass_r.at[i - 1, c])


def layer_kernel(names, *refs):
    r = types.SimpleNamespace(**dict(zip(names, refs)))
    place = Place()
    y = place.y
    tokens, features = r.student.shape
    part = r.projector.shape[1]
    units = r.down.shape[0]
    block = 2 * r.rows.shape[3]
    piece = r.step.shape[0]
    share_rows = tokens // NY
    chunks = part // WIDTH
    f32, bf16 = jnp.float32, jnp.bfloat16
    mine = place.member()
    steps = len(UNITS)
    after, ahead = lax.rem(y + 1, NY), lax.rem(y + NY - 1, NY)

    capacity = block // NZ
    fours = NZ // 2
    rows = block // 2
    far_share = lax.rem(y + 2, NY)
    loads = [
        pltpu.make_async_copy(
            r.teacher_in.at[:, part_of(y, part)], r.tok.at[0, cut_of(DISTANCES.index(0), tokens)], r.load.at[0]
        ),
        pltpu.make_async_copy(
            r.teacher_in.at[:, part_of(far_share, part)], r.tok.at[1, cut_of(DISTANCES.index(0), tokens)], r.load.at[1]
        ),
        pltpu.make_async_copy(r.projector, r.proj, r.load.at[2]),
        pltpu.make_async_copy(r.gate_up, r.gates, r.load.at[3]),
        pltpu.make_async_copy(r.down.at[:, part_of(y, part)], r.down_all.at[0], r.load.at[4]),
    ]
    barrier, peers = greet(place)
    for load in loads:
        load.start()
    gain = r.gain[...]
    feat = norm(r.student[...].astype(f32))[1] * gain
    r.feat[...] = feat.astype(bf16)
    pl.semaphore_wait(barrier, peers)
    sends = []

    def send(*args):
        copy = remote(*args)
        copy.start()
        sends.append(copy)

    def landed(ref, send_sem, recv_sem):
        remote(ref, ref, send_sem, recv_sem, place.at(), y).wait_recv()

    members = [(dx, dk) for dx in range(NX) for dk in range(2) if dx or dk]

    half = part // 2

    def ring_slot(q, way, hops, c):
        d = hops if way == 0 else (NZ - hops) % NZ
        return r.tok.at[q, cut_of(DISTANCES.index(d), tokens), cut_of(c, half)]

    def ring_send(q, way, hops, c):
        i = way * NZ + hops * 2 + c
        send(
            ring_slot(q, way, hops, c),
            ring_slot(q, way, hops + 1, c),
            r.tok_s.at[q, i],
            r.tok_r.at[q, i],
            place.at(dz=1 if way == 0 else NZ - 1),
            y,
        )

    def ring_start(q):
        for c in range(2):
            for way in range(2):
                ring_send(q, way, 0, c)

    def ring_step(q, hops):
        for c in range(2):
            for way in range(2):
                if hops < NZ // 2 or c == way:
                    i = way * NZ + (hops - 1) * 2 + c
                    landed(ring_slot(q, way, hops, c), r.tok_s.at[q, i], r.tok_r.at[q, i])
                if hops < NZ // 2 - 1 or (hops == NZ // 2 - 1 and c == way):
                    ring_send(q, way, hops, c)

    for dz in range(1, NZ):
        send(
            r.meta.at[lax.rem(place.z + dz, NZ)],
            r.metas.at[dz],
            r.meta_s.at[dz - 1],
            r.meta_r.at[dz - 1],
            place.at(dz=dz),
            y,
        )
    loads[0].wait()
    ring_start(0)
    for dy in (2, 1, 3):
        to = lax.rem(y + dy, NY)
        send(
            r.down.at[:, part_of(to, part)],
            r.down_all.at[dy],
            r.down_s.at[dy - 1],
            r.down_r.at[dy - 1],
            place.at(),
            to,
        )
    r.metas[0] = r.meta[place.z]
    number = lax.broadcasted_iota(jnp.int32, (rows, tokens), 0).astype(f32)

    def expert_at(i):
        return pl.ds(place.member(i // 2, i % 2), 1)

    def weigh(j):
        group, i = j // fours, j % fours
        d = DISTANCES[j]
        pieces = []
        for o in range(OCT):
            code = r.metas[d, 0, expert_at(o), :] + float(i * capacity)
            pieces.append(jnp.where(number == code, r.metas[d, 1, expert_at(o), :], 0.0))
        r.spread[group, cut_of(i, tokens), :] = jnp.concatenate(pieces, axis=0).T.astype(bf16)

    ring_step(0, 1)
    for dz in range(1, NZ):
        landed(r.metas.at[dz], r.meta_s.at[dz - 1], r.meta_r.at[dz - 1])
    for i in range(fours):
        weigh(i)

    ring_step(0, 2)

    for x in range(NX):
        for z in range(NZ):
            for k in range(2):
                at = ((x * NZ + z) * 2 + k) * piece
                if at % tokens == 0:
                    turned = feat[:, at : at + tokens].T.astype(bf16)
                r.slab[x * 2 + k, z * piece : (z + 1) * piece, :] = turned[
                    at % tokens : at % tokens + piece
                ]
    ring_step(0, 3)
    loads[1].wait()
    ring_start(1)
    for i in range(fours, NZ):
        weigh(i)
    ring_step(0, 4)

    def select_rows(q, u):
        group, dx = u // NX, u % NX
        for i in range(fours):
            d = DISTANCES[group * fours + i]
            pieces = []
            for dk in range(2):
                code = r.metas[d, 0, expert_at(2 * dx + dk), :] + float(i * capacity)
                pieces.append(jnp.where(number == code, 1.0, 0.0))
            r.select[:, cut_of(i, tokens)] = jnp.concatenate(pieces, axis=0).astype(bf16)
        picked = dot(r.select[...], r.tok[q, cut_of(group, fours * tokens)])
        for dk in range(2):
            if dx or dk:
                r.out[q, u, dk] = picked[cut_of(dk, rows)].astype(bf16)
                send(
                    r.out.at[q, u, dk],
                    r.rows.at[2 * q, u, dk],
                    r.x_s.at[q, 2 * u + dk],
                    r.x_r.at[q, 2 * u + dk],
                    place.at(dx=dx, dk=dk),
                    y,
                )
            else:
                r.rows[2 * q, u, dk] = picked[cut_of(dk, rows)].astype(bf16)

    def rows_landed(q, u):
        for dk in range(2):
            if u % NX or dk:
                at = r.rows.at[2 * q, u, dk]
                landed(at, r.x_s.at[q, 2 * u + dk], r.x_r.at[q, 2 * u + dk])

    def pass_rows(j):
        u = UNITS[j]
        rows_landed(0, u)
        send(r.rows.at[0, u], r.rows.at[1, u], r.up_s.at[u], r.up_r.at[u], place.at(), after)
        send(r.rows.at[0, u], r.rows.at[3, u], r.low_s.at[u], r.low_r.at[u], place.at(), ahead)

    for j in range(steps):
        select_rows(0, UNITS[j])
        if j % 2 == 1:
            ring_step(1, (j + 1) // 2)
        if j >= 1:
            pass_rows(j - 1)
    for j in range(steps):
        select_rows(1, UNITS[j])
        if j == 0:
            pass_rows(steps - 1)

    slot = part_of(mine, tokens)
    for i, (dx, dk) in enumerate(members):
        send(
            r.slab.at[place.member(dx, dk)],
            r.slabs.at[:, slot],
            r.slab_s.at[i],
            r.slab_r.at[i],
            place.at(dx=dx, dk=dk),
            y,
        )
    r.slabs[:, slot] = r.slab[mine]
    for load in loads[2:]:
        load.wait()

    def first_product(j):
        i = UNITS[j]
        rows_landed(1, i)
        landed(r.rows.at[1, i], r.up_s.at[i], r.up_r.at[i])
        landed(r.rows.at[3, i], r.low_s.at[i], r.low_r.at[i])
        out = jnp.zeros((block, 2 * units), f32)
        for ry in range(NY):
            share = lax.rem(y + NY - ry, NY)
            out += dot(r.rows[ry, i].reshape(block, part), r.gates[part_of(share, part), :])
        gate, up = out[:, :units], out[:, units:]
        r.hidden[0, i] = (gate / (1.0 + jnp.exp(-gate)) * up).astype(bf16)
        for dy, to in ((1, after), (3, ahead)):
            send(
                r.hidden.at[0, i], r.hidden.at[dy, i], r.hid_s.at[dy, i], r.hid_r.at[dy, i], place.at(), to
            )

    def relay_hidden(j):
        i = UNITS[j]
        for dy in (1, 3):
            landed(r.hidden.at[dy, i], r.hid_s.at[dy, i], r.hid_r.at[dy, i])
        source, to = (1, after) if j % 2 == 0 else (3, ahead)
        send(r.hidden.at[source, i], r.hidden.at[2, i], r.hid_s.at[2, i], r.hid_r.at[2, i], place.at(), to)

    def second_product(j):
        u = UNITS[j]
        dx = u % NX
        landed(r.hidden.at[2, u], r.hid_s.at[2, u], r.hid_r.at[2, u])
        out = jnp.zeros((block, part), f32)
        for ry in range(NY):
            out += dot(r.hidden[ry, u], r.down_all[ry])
        for dk in range(2):
            if dx or dk:
                r.back[u, dk] = out[cut_of(dk, rows)].astype(bf16)
                send(
                    r.back.at[u, dk],
                    r.home.at[2 * u + dk],
                    r.ret_s.at[2 * u + dk],
                    r.ret_r.at[2 * u + dk],
                    place.at(dx=NX - dx, dk=dk),
                    y,
                )
            else:
                r.home[2 * u + dk] = out[cut_of(dk, rows)].astype(bf16)

    def came_home(group):
        for u in range(group * NX, (group + 1) * NX):
            for dk in range(2):
                if u % NX or dk:
                    landed(r.home.at[2 * u + dk], r.ret_s.at[2 * u + dk], r.ret_r.at[2 * u + dk])

    def combine(group, n):
        r.total[n, cut_of(group, fours * tokens), :] = dot(
            r.spread[group], r.home[cut_of(group, OCT), :, cut_of(n, WIDTH)].reshape(NX * block, WIDTH)
        )

    def sum_hop(n, way, left):
        d = left if way == 0 else NZ - left
        here = r.total[n, cut_of(DISTANCES.index(d), tokens), :]
        if left < NZ // 2 - 1 or (left == NZ // 2 - 1 and n % 2 == way):
            i = left * chunks + n
            landed(r.sum_in.at[way, left, n], r.sum_s.at[way, i], r.sum_r.at[way, i])
            here += r.sum_in[way, left, n].astype(f32)
        r.sum_out[way, left - 1, n] = here.astype(bf16)
        i = (left - 1) * chunks + n
        send(
            r.sum_out.at[way, left - 1, n],
            r.sum_in.at[way, left - 1, n],
            r.sum_s.at[way, i],
            r.sum_r.at[way, i],
            place.at(dz=NZ - 1 if way == 0 else 1),
            y,
        )

    for j in range(steps + 2):
        if j < steps:
            first_product(j)
        if 0 <= j - 1 < steps:
            relay_hidden(j - 1)
        if j == 1:
            for n in range(chunks):
                r.dense[:, cut_of(n, WIDTH)] = dot(r.feat[...], r.proj[:, cut_of(n, WIDTH)])
        if j == 2:
            for dy in range(1, NY):
                landed(r.down_all.at[dy], r.down_s.at[dy - 1], r.down_r.at[dy - 1])
        if 0 <= j - 2 < steps:
            second_product(j - 2)
        if j == NX + 2:
            came_home(0)
            for n in range(chunks):
                combine(0, n)
                sum_hop(n, n % 2, 4)
        if j == NX + 3:
            for n in range(chunks):
                sum_hop(n, 0, 3)
                sum_hop(n, 1, 3)
        if j == NX + 4:
            for n in range(chunks):
                sum_hop(n, 0, 2)
    came_home(1)

    res = Gather(
        place, send, landed, r.residue, tokens, WIDTH, (r.res_s, r.res_r, r.resf_s, r.resf_r)
    )
    def sum_rows(n):
        res.finish(n)
        grad = dot(r.slabs[...], r.residue[:, cut_of(n, WIDTH)]).reshape(NZ, piece, WIDTH)
        r.grad[n] = grad.astype(bf16)
        r.own_grad[n] = grad
        for dz in (4, 3, 5, 2, 6, 1, 7):
            send(
                r.grad.at[n, lax.rem(place.z + dz, NZ)],
                r.grads.at[dz - 1, n],
                r.grad_s.at[dz - 1, n],
                r.grad_r.at[dz - 1, n],
                place.at(dz=dz),
                y,
            )

    for i, (dx, dk) in enumerate(members):
        at = part_of(place.member(NX - dx, dk), tokens)
        landed(r.slabs.at[:, at], r.slab_s.at[i], r.slab_r.at[i])
    for wave in range(chunks + 4):
        for n in reversed(range(chunks)):
            stage = wave - n
            if stage == 0:
                combine(1, n)
                sum_hop(n, 1, 2)
            elif stage == 1:
                sum_hop(n, 0, 1)
                sum_hop(n, 1, 1)
            elif stage == 2:
                teacher = r.total[n, cut_of(DISTANCES.index(0), tokens), :]
                for way in range(2):
                    landed(r.sum_in.at[way, 0, n], r.sum_s.at[way, n], r.sum_r.at[way, n])
                    teacher += r.sum_in[way, 0, n].astype(f32)
                cut = cut_of(n, WIDTH)
                r.residue[slot, cut] = (r.dense[:, cut] - teacher).astype(bf16)
                res.start(n)
            elif stage == 3:
                res.onward(n)
            elif stage == 4:
                sum_rows(n)
        if wave == chunks + 1:
            for n in range(features // WIDTH):
                r.part[:, cut_of(n, WIDTH)] = lax.dot_general(
                    r.residue[slot, :],
                    r.proj[cut_of(n, WIDTH), :],
                    (((1,), (1,)), ((), ())),
                    preferred_element_type=f32,
                ).astype(bf16)
            for dy in (2, 1, 3):
                to = lax.rem(y + dy, NY)
                send(
                    r.part.at[part_of(to, share_rows)],
                    r.parts.at[dy - 1],
                    r.part_s.at[dy - 1],
                    r.part_r.at[dy - 1],
                    place.at(),
                    to,
                )


    own_rows = part_of(y, share_rows)
    feat_grad = r.part[own_rows, :].astype(f32)
    for dy in range(1, NY):
        landed(r.parts.at[dy - 1], r.part_s.at[dy - 1], r.part_r.at[dy - 1])
        feat_grad += r.parts[dy - 1].astype(f32)
    inv, normed = norm(r.student[own_rows, :].astype(f32))
    scaled = feat_grad * gain
    r.d_own[...] = (
        inv * (scaled - normed * jnp.mean(scaled * normed, axis=1, keepdims=True))
    ).astype(bf16)
    for dy in (2, 1, 3):
        to = lax.rem(y + dy, NY)
        send(r.d_own, r.d_all.at[dy - 1], r.d_s.at[dy - 1], r.d_r.at[dy - 1], place.at(), to)
    r.d[own_rows, :] = r.d_own[...]

    for n in range(chunks):
        total = r.own_grad[n, place.z]
        for dz in (1, 7, 2, 6, 3, 5, 4):
            landed(r.grads.at[dz - 1, n], r.grad_s.at[dz - 1, n], r.grad_r.at[dz - 1, n])
            total += r.grads[dz - 1, n].astype(f32)
        cut = cut_of(n, WIDTH)
        r.step[:, cut] = total * lax.rsqrt(
            beta_two * r.moment[:, cut] + (1.0 - beta_two) * total * total
        )
    for dy in range(1, NY):
        landed(r.d_all.at[dy - 1], r.d_s.at[dy - 1], r.d_r.at[dy - 1])
        r.d[part_of(lax.rem(y + NY - dy, NY), share_rows), :] = r.d_all[dy - 1]
    for copy in sends:
        copy.wait_send()


def layer(teacher_in, meta, gate_up, down, student_in, norm_gain, projector, second_moment, capacity):
    tokens, features = student_in.shape
    part = projector.shape[1]
    units = down.shape[0]
    block = OCT * capacity
    piece = second_moment.shape[0]
    share_rows = tokens // NY
    chunks = part // WIDTH
    bf16, f32 = jnp.bfloat16, jnp.float32
    vmem, anywhere = pl.BlockSpec(memory_space=pltpu.VMEM), pl.BlockSpec(memory_space=pl.ANY)
    inputs = dict(
        teacher_in=(teacher_in, anywhere),
        meta=(meta, vmem),
        gate_up=(gate_up, anywhere),
        down=(down, anywhere),
        student=(student_in, vmem),
        gain=(norm_gain.reshape(1, -1), vmem),
        projector=(projector, anywhere),
        moment=(second_moment, vmem),
    )
    outputs = dict(
        d=jax.ShapeDtypeStruct((tokens, features), bf16),
        step=jax.ShapeDtypeStruct(second_moment.shape, f32),
    )
    buffers = dict(
        proj=(projector.shape, bf16),
        gates=(gate_up.shape, bf16),
        tok=((2, NZ * tokens, part), bf16),
        metas=(meta.shape, f32),
        select=((block, NZ // 2 * tokens), bf16),
        spread=((2, NZ // 2 * tokens, NX * block), bf16),
        out=((2, OCT, 2, block // 2, part), bf16),
        rows=((NY, OCT, 2, block // 2, part), bf16),
        hidden=((NY, NZ, block, units), bf16),
        down_all=((NY, units, part), bf16),
        back=((OCT, 2, block // 2, part), bf16),
        home=((2 * OCT, block // 2, part), bf16),
        total=((chunks, NZ * tokens, WIDTH), f32),
        sum_out=((2, NZ // 2, chunks, tokens, WIDTH), bf16),
        sum_in=((2, NZ // 2, chunks, tokens, WIDTH), bf16),
        feat=((tokens, features), bf16),
        dense=((tokens, part), f32),
        slab=((OCT, NZ * piece, tokens), bf16),
        slabs=((NZ * piece, OCT * tokens), bf16),
        residue=((OCT * tokens, part), bf16),
        part=((tokens, features), bf16),
        parts=((NY - 1, share_rows, features), bf16),
        d_own=((share_rows, features), bf16),
        d_all=((NY - 1, share_rows, features), bf16),
        grad=((chunks, NZ, piece, WIDTH), bf16),
        grads=((NZ - 1, chunks, piece, WIDTH), bf16),
        own_grad=((chunks, NZ, piece, WIDTH), f32),
    )
    flights = dict(
        meta=(NZ - 1,),
        tok=(2, 2 * NZ),
        down=(NY - 1,),
        x=(2, 2 * OCT),
        up=(OCT,),
        low=(OCT,),
        hid=(NY, OCT),
        ret=(2 * OCT,),
        sum=(2, NZ // 2 * chunks),
        slab=(OCT - 1,),
        res=(4, chunks),
        resf=(3, chunks),
        part=(NY - 1,),
        d=(NY - 1,),
        grad=(NZ - 1, chunks),
    )
    dma = pltpu.SemaphoreType.DMA
    pairs = {f"{name}_{end}": dma(shape) for name, shape in flights.items() for end in "sr"}
    names = (*inputs, *outputs, *buffers, *pairs, "load")
    return pl.pallas_call(
        functools.partial(layer_kernel, names),
        out_shape=tuple(outputs.values()),
        in_specs=[spec for _, spec in inputs.values()],
        out_specs=[vmem] * len(outputs),
        scratch_shapes=[pltpu.VMEM(*b) for b in buffers.values()] + [*pairs.values(), dma((5,))],
        compiler_params=pltpu.CompilerParams(
            collective_id=0, has_side_effects=True, vmem_limit_bytes=60 << 20
        ),
    )(*(value for value, _ in inputs.values()))


def slot_maps(routes, route_weights, experts):
    tokens = routes.shape[0]
    named = routes[:, :, None] == jnp.arange(experts, dtype=jnp.int32)[None, None, :]
    member = jnp.any(named, axis=1)
    weight = jnp.sum(jnp.where(named, route_weights[:, :, None], 0.0), axis=1)
    earlier = jnp.tril(jnp.ones((tokens, tokens), jnp.bfloat16), -1)
    before = jnp.dot(earlier, member.astype(jnp.bfloat16), preferred_element_type=jnp.float32)
    position = jnp.where(member, before.astype(jnp.int32), -1)
    return position.T, weight.T


def per_device(
    teacher_in,
    routes,
    route_weights,
    expert_gate_up,
    expert_down,
    student_in,
    norm_gain,
    projector,
    second_moment,
):
    tokens_here = teacher_in.shape[0]
    top_count = routes.shape[1]
    experts = lax.axis_size("expert")
    capacity = min(tokens_here, tokens_here * top_count * 9 // (8 * experts))
    position, weight = slot_maps(routes, route_weights, experts)
    code = jnp.where(position >= 0, position, -tokens_here * experts)
    meta = jnp.stack([code.astype(jnp.float32), weight])
    meta = meta.reshape(2, NX, NZ, 2, tokens_here).transpose(2, 0, 1, 3, 4)
    meta = meta.reshape(NZ, 2, OCT, tokens_here)
    gate_up = expert_gate_up.reshape(expert_gate_up.shape[1], -1)
    return layer(
        teacher_in,
        meta,
        gate_up,
        expert_down[0],
        student_in,
        norm_gain,
        projector,
        second_moment,
        capacity,
    )


def solution(mesh):
    placed = (
        P("expert", None),
        P("expert", None),
        P("expert", None),
        P("expert", None, None, "fsdp"),
        P("expert", "fsdp", None),
        P("expert", None),
        P(),
        P(None, "fsdp"),
        P("expert", "fsdp"),
    )
    return jax.shard_map(
        per_device,
        mesh=mesh,
        in_specs=placed,
        out_specs=(P("expert", None), P("expert", "fsdp")),
        check_vma=False,
    )
```
